128 devices in a mesh: lon: 32 (over x_hi, z, y), lat: 4 (over x_lo, core).
Axes of the slice: x: 4 (x_hi: 2, x_lo: 2; x = x_hi * 2 + x_lo), y: 4, z: 4, core: 2. Of those that a mesh axis runs over, the one named last changes fastest.
Arguments:
- right_side: float32 [20, 1024, 4096], P(None, 'lat', 'lon'), may hold values from -6 to 6
- helmholtz: float32 [20, 1024, 4096], P(None, 'lat', 'lon'), may hold values from 0.3 to 3
- coupling: float32 [19, 1024, 4096], P(None, 'lat', 'lon'), may hold values from 1 to 10
Outputs:
- solution: float32 [20, 1024, 4096], P(None, 'lat', 'lon')
- residual: float32 [20, 1024, 4096], P(None, 'lat', 'lon')
The draws below stay inside these ranges and needn't reach their ends.
All inputs are finite; a program needn't handle non-finite values.
Results may differ from the reference program's by a relative error of at most 0.0003.
Values sent between devices are 32-bit elements; how exact they have to be, the bound alone decides.
No kernel may reach another device: no remote copies, remote signals or barrier semaphores. Data moves between devices by JAX's collectives and lax.ppermute only.
A program may use at most 128 MiB of HBM per device.

```python
import math
import jax
import jax.numpy as jnp

K = 20
ITERS = 3
NLON = 4096
NLAT = 1024


def level_of(rng, extent, pieces, least, largest):
    level, own = 1.0, jax.random.fold_in(rng, 6)
    for axis_at, blocks in pieces:
        draws = jnp.exp(jax.random.uniform(jax.random.fold_in(own, axis_at), (blocks,), jnp.float32, least / len(pieces), largest / len(pieces)))
        level = level * jnp.repeat(draws, extent[axis_at] // blocks).reshape([-1 if axis == axis_at else 1 for axis in range(len(extent))])
    return level


def scatter_about(rng, dims, spread, most, cuts=(), held_as=jnp.bfloat16):
    entries = spread * jax.random.normal(rng, dims, jnp.float32)
    if cuts:
        entries = entries * level_of(rng, dims, cuts, -0.22, 0.18)
    return jnp.clip(entries, -most, most).astype(held_as)


def setup_inputs(seed: int = 0) -> dict:
    splits = jax.random.split(jax.random.key(seed), 4)
    return {
        "right_side": scatter_about(splits[0], (K, NLAT, NLON), 1.0, 6.0, ((1, 4), (2, 32)), jnp.float32),
        "helmholtz": jnp.clip(jnp.exp(math.log(3.0) - 2.3025851 * jax.random.uniform(splits[1], (K, NLAT, NLON), jnp.float32) ** level_of(splits[1], (K, NLAT, NLON), ((1, 4), (2, 32)), -0.2, 0.2)), 0.3, 3.0),
        "coupling": jnp.clip(jnp.exp(math.log(10.0) - 2.3025851 * jax.random.uniform(splits[2], (K - 1, NLAT, NLON), jnp.float32) ** level_of(splits[2], (K - 1, NLAT, NLON), ((1, 4), (2, 32)), -0.2, 0.2)), 1.0, 10.0),
    }


def cosines(rows, total_rows):
    latitude = -0.5 * math.pi + (rows + 0.5) * (math.pi / total_rows)
    return jnp.maximum(jnp.cos(latitude), 0.5)


def factors(helmholtz, coupling, cosine, north_face, south_face, lon_coeff):
    zero_level = jnp.zeros_like(coupling[:1])
    vertical_sum = jnp.concatenate([coupling, zero_level], 0) + jnp.concatenate([zero_level, coupling], 0)
    diagonal = cosine * helmholtz + 2.0 * lon_coeff / cosine + north_face + south_face + cosine * vertical_sum
    offdiag = -cosine * coupling
    levels = diagonal.shape[0]
    inverse = []
    ratios = []
    pivot = diagonal[0]
    for layer in range(levels):
        if layer > 0:
            pivot = diagonal[layer] - offdiag[layer - 1] * ratios[layer - 1]
        inverse.append(1.0 / pivot)
        if layer < levels - 1:
            ratios.append(offdiag[layer] * (1.0 / pivot))
    return offdiag, inverse, ratios


def solve_lines(values, offdiag, inverse, ratios):
    levels = len(inverse)
    forward = [values[0] * inverse[0]]
    for layer in range(1, levels):
        forward.append((values[layer] - offdiag[layer - 1] * forward[layer - 1]) * inverse[layer])
    result = [None] * levels
    result[levels - 1] = forward[levels - 1]
    for layer in range(levels - 2, -1, -1):
        result[layer] = forward[layer] - ratios[layer] * result[layer + 1]
    return jnp.stack(result)


def combine(field, east_cells, west_cells, north_cells, south_cells, helmholtz, coupling, cosine, north_face, south_face, lon_coeff):
    zero_level = jnp.zeros_like(field[:1])
    vertical_flux = coupling * (field[:-1] - field[1:])
    vertical = jnp.concatenate([vertical_flux, zero_level], 0) - jnp.concatenate([zero_level, vertical_flux], 0)
    result = cosine * helmholtz * field + (lon_coeff / cosine) * (2.0 * field - east_cells - west_cells)
    result = result + north_face * (field - north_cells) + south_face * (field - south_cells)
    return result + cosine * vertical


def operate(field, helmholtz, coupling, cosine, north_face, south_face, lon_coeff):
    east_cells = jnp.roll(field, -1, axis=2)
    west_cells = jnp.roll(field, 1, axis=2)
    north_pole = jnp.roll(field[:, -1:, :], NLON // 2, axis=2)
    south_pole = jnp.roll(field[:, :1, :], NLON // 2, axis=2)
    north_cells = jnp.concatenate([field[:, 1:, :], north_pole], 1)
    south_cells = jnp.concatenate([south_pole, field[:, :-1, :]], 1)
    return combine(field, east_cells, west_cells, north_cells, south_cells, helmholtz, coupling, cosine, north_face, south_face, lon_coeff)


def reference(right_side, helmholtz, coupling):
    rows = jnp.arange(NLAT).astype(jnp.float32)
    cosine = cosines(rows, NLAT)
    below = cosines(jnp.maximum(rows - 1.0, 0.0), NLAT)
    above = cosines(jnp.minimum(rows + 1.0, NLAT - 1.0), NLAT)
    south_face = ((cosine + below) * 0.5).reshape(1, -1, 1)
    north_face = ((cosine + above) * 0.5).reshape(1, -1, 1)
    cosine = cosine.reshape(1, -1, 1)
    lon_coeff = (NLON / (2.0 * NLAT)) ** 2
    offdiag, inverse, ratios = factors(helmholtz, coupling, cosine, north_face, south_face, lon_coeff)

    def apply_operator(field):
        return operate(field, helmholtz, coupling, cosine, north_face, south_face, lon_coeff)

    def smooth(values):
        return solve_lines(values, offdiag, inverse, ratios)

    solution = jnp.zeros_like(right_side)
    residual = right_side
    smoothed = smooth(residual)
    image_smooth = apply_operator(smoothed)
    energy = jnp.sum(smoothed * image_smooth)
    direction = smoothed
    image_dir = image_smooth
    for iteration in range(ITERS):
        back_image = smooth(image_dir)
        step_length = energy / jnp.sum(image_dir * back_image)
        solution = solution + step_length * direction
        residual = residual - step_length * image_dir
        smoothed = smoothed - step_length * back_image
        if iteration < ITERS - 1:
            image_smooth = apply_operator(smoothed)
            energy_next = jnp.sum(smoothed * image_smooth)
            step_ratio = energy_next / energy
            direction = smoothed + step_ratio * direction
            image_dir = image_smooth + step_ratio * image_dir
            energy = energy_next
    return solution, residual
```

```python
import functools
import math

import jax
import jax.numpy as jnp
from jax import lax
from jax.experimental import pallas as pl
from jax.experimental.pallas import tpu as pltpu
from jax.sharding import PartitionSpec as P

LEVELS = 20
ROWS = 256
LANES = 128
TOTAL_ROWS = 1024
LON_COEFF = 4.0
TILES = ROWS // 8 + 2
EXTENDED = 8 * TILES + 16
STACKED = 3 * LEVELS - 1
AT_H = LEVELS
AT_C = 2 * LEVELS
CHUNKS = 8
AXES = ("lon", "lat")
F32 = jnp.float32
MIB = 1 << 20


def swap(x, partner):
    return lax.ppermute(x, AXES, [(i, partner(i)) for i in range(128)])


def lat_even(i):
    return i ^ 1


def lat_odd(i):
    lon, lat = i >> 2, i & 3
    if lat in (1, 2):
        return (lon << 2) | (3 - lat)
    return ((lon ^ 16) << 2) | lat


def lon_even(i):
    return i ^ 4


def lon_odd(i):
    lon, lat = i >> 2, i & 3
    other = (lon + 1) % 32 if lon % 2 else (lon - 1) % 32
    return (other << 2) | lat


def lane_index():
    return lax.broadcasted_iota(jnp.int32, (8, LANES), 1)


def sub_index():
    return lax.broadcasted_iota(jnp.int32, (8, LANES), 0)


def capped_cosine(row):
    angle = (row + 0.5) * (math.pi / TOTAL_ROWS) - 0.5 * math.pi
    square = angle * angle
    value = jnp.full_like(row, 0.0)
    for n in range(8, -1, -1):
        value = value * square + (-1.0) ** n / math.factorial(2 * n)
    return jnp.maximum(value, 0.5)


def row_terms(row):
    here = capped_cosine(row)
    return (
        here,
        LON_COEFF / here,
        (here + capped_cosine(row + 1.0)) * 0.5,
        (here + capped_cosine(row - 1.0)) * 0.5,
    )


def eliminate(terms, right, helm, coup, store):
    cosine, over, north, south = terms
    fixed = 2.0 * over + north + south
    forward = []
    ratios = []
    below = None
    for k in range(LEVELS):
        scaled = cosine * coup(k) if k < LEVELS - 1 else None
        pivot = cosine * helm(k) + fixed
        if scaled is not None:
            pivot = pivot + scaled
        if below is not None:
            pivot = pivot + below
            pivot = pivot - below * ratios[-1]
        inverse = 1.0 / pivot
        value = right(k)
        if below is not None:
            value = value + below * forward[-1]
        forward.append(value * inverse)
        ratio = None
        if scaled is not None:
            ratio = scaled * inverse
            ratios.append(ratio)
        store(k, scaled, inverse, ratio)
        below = scaled
    return forward, ratios


def packed_edges(read, lane):
    last = jnp.zeros((8, LANES), F32)
    first = jnp.zeros((8, LANES), F32)
    group = lane // 3
    for t in range(1, TILES - 1):
        turned = pltpu.roll(read(t), 3 * t + 3, axis=1)
        last = jnp.where(group == t, turned, last)
        first = jnp.where(group == t + 1, turned, first)
    return last, first


def edge_rows_kernel(b_lo, b_hi, h_lo, h_hi, c_lo, c_hi, a_ref, o_ref):
    even = lax.axis_index("lat") % 2 == 0
    for at, count, lo, hi in (
        (0, LEVELS, b_lo, b_hi),
        (AT_H, LEVELS, h_lo, h_hi),
        (AT_C, LEVELS - 1, c_lo, c_hi),
    ):
        low, high = lo[...], hi[...]
        a_ref[pl.ds(at, count)] = jnp.where(even, high, low)
        o_ref[pl.ds(at, count)] = jnp.where(even, low, high)


def first_kernel(
    b_hbm, h_hbm, c_hbm, b_ref, scaled_ref, inverse_ref, ratio_ref, x_ref, terms_ref, last_ref,
    first_ref, h_ref, c_ref, sems
):
    step = ROWS // CHUNKS

    def copy(i, n):
        src = (b_hbm, h_hbm, c_hbm)[i]
        dst = (b_ref, h_ref, c_ref)[i]
        rows = pl.ds(n * step, step)
        return pltpu.make_async_copy(src.at[:, rows, :], dst.at[:, rows, :], sems.at[i, n])

    for n in range(CHUNKS):
        for i in range(3):
            copy(i, n).start()
    base = lax.axis_index("lat") * ROWS
    lane = lane_index()
    sub = sub_index()

    def row_term(t, carry):
        row = (base + 8 * t - 8 + sub).astype(F32)
        for i, term in enumerate(row_terms(row)):
            terms_ref[i, pl.ds(pl.multiple_of(8 * t, 8), 8), :] = term
        return carry

    lax.fori_loop(0, TILES, row_term, 0)
    for n in range(CHUNKS):
        for i in range(3):
            copy(i, n).wait()

        def tile(t, carry):
            at = pl.ds(pl.multiple_of(8 * t - 8, 8), 8)
            wide = pl.ds(pl.multiple_of(8 * t + 8, 8), 8)
            terms = [terms_ref[i, pl.ds(pl.multiple_of(8 * t, 8), 8), :] for i in range(4)]

            def store(k, scaled, inverse, ratio):
                inverse_ref[k, wide, :] = inverse
                if scaled is not None:
                    scaled_ref[k, wide, :] = scaled
                    ratio_ref[k, wide, :] = ratio

            forward, ratios = eliminate(
                terms,
                lambda k: b_ref[k, at, :],
                lambda k: h_ref[k, at, :],
                lambda k: c_ref[k, at, :],
                store,
            )
            value = forward[-1]
            x_ref[LEVELS - 1, wide, :] = value
            for k in range(LEVELS - 2, -1, -1):
                value = forward[k] + ratio_ref[k, wide, :] * value
                x_ref[k, wide, :] = value
            return carry

        lax.fori_loop(1 + n * step // 8, 1 + (n + 1) * step // 8, tile, 0)

    def pack(source, at, count):
        def level(k, carry):
            last, first = packed_edges(lambda t: source[k, pl.ds(8 * t - 8, 8), :], lane)
            last_ref[at + k] = last
            first_ref[at + k] = first
            return carry

        lax.fori_loop(0, count, level, 0)

    pack(b_ref, 0, LEVELS)
    pack(h_ref, AT_H, LEVELS)
    pack(c_ref, AT_C, LEVELS - 1)


def edge_lanes_kernel(a_ref, o_ref, last_ref, first_ref, south_ref, north_ref, e_ref, d_ref):
    lat = lax.axis_index("lat")
    lat_is_even = lat % 2 == 0
    lon_is_even = lax.axis_index("lon") % 2 == 0
    polar = jnp.logical_or(lat == 0, lat == 3)
    lane = lane_index()
    sub = sub_index()
    group = lane // 3

    def level(j, carry):
        near = a_ref[j]
        far = o_ref[j]
        flipped = far
        for s in (0, 1, 2, 5, 6, 7):
            flipped = jnp.where(sub == s, jnp.broadcast_to(far[7 - s : 8 - s], (8, LANES)), flipped)
        far = jnp.where(polar, flipped, far)
        south = jnp.where(lat_is_even, far, near)
        north = jnp.where(lat_is_even, near, far)
        south_ref[j] = south
        north_ref[j] = north
        last, first = last_ref[j], first_ref[j]
        for t, value in ((0, south), (TILES - 1, north)):
            turned = pltpu.roll(value, 3 * t + 3, axis=1)
            last = jnp.where(group == t, turned, last)
            first = jnp.where(group == t + 1, turned, first)
        first = pltpu.roll(first, LANES - 3, axis=1)
        e_ref[j] = jnp.where(lon_is_even, last, first)
        d_ref[j] = jnp.where(lon_is_even, first, last)
        return carry

    lax.fori_loop(0, STACKED, level, 0, unroll=2)


def middle_kernel(
    b_ref, scaled_in, inverse_in, ratio_in, x0_in, terms_ref, south_ref, north_ref, e_ref, d_ref,
    scaled_ref, inverse_ref, ratio_ref, x0_ref, x1_ref, x2_ref, y1_ref, y2_ref, y3_ref, sums_ref,
    left_ref, right_ref, joint_ref, edge_ref, strip_ref
):
    del scaled_in, inverse_in, ratio_in, x0_in
    base = lax.axis_index("lat") * ROWS
    lon_is_even = lax.axis_index("lon") % 2 == 0
    lane = lane_index()
    sub = sub_index()
    slot = lane % 3
    group = lane // 3

    for t, source in ((0, south_ref), (TILES - 1, north_ref)):
        wide = pl.ds(8 * t + 8, 8)
        terms = [terms_ref[i, pl.ds(8 * t, 8), :] for i in range(4)]

        def store(k, scaled, inverse, ratio, wide=wide):
            inverse_ref[k, wide, :] = inverse
            if scaled is not None:
                scaled_ref[k, wide, :] = scaled
                ratio_ref[k, wide, :] = ratio

        forward, ratios = eliminate(
            terms,
            lambda k, source=source: source[k],
            lambda k, source=source: source[AT_H + k],
            lambda k, source=source: source[AT_C + k],
            store,
        )
        value = forward[-1]
        x0_ref[LEVELS - 1, wide, :] = value
        for k in range(LEVELS - 2, -1, -1):
            value = forward[k] + ratios[k] * value
            x0_ref[k, wide, :] = value

    strip_row = (base + 8 * group - 8 + sub).astype(F32)
    strip_terms = row_terms(strip_row)
    for side, out in ((0, left_ref), (1, right_ref)):

        def received(j, side=side):
            even, odd = (d_ref, e_ref) if side == 0 else (e_ref, d_ref)
            return jnp.where(lon_is_even, even[j], odd[j])

        def store(k, scaled, inverse, ratio, side=side):
            strip_ref[side, 1, k] = inverse
            if scaled is not None:
                strip_ref[side, 0, k] = scaled
                strip_ref[side, 2, k] = ratio

        forward, ratios = eliminate(
            strip_terms,
            received,
            lambda k: received(AT_H + k),
            lambda k: received(AT_C + k),
            store,
        )
        value = forward[-1]
        out[LEVELS - 1] = value
        for k in range(LEVELS - 2, -1, -1):
            value = forward[k] + ratios[k] * value
            out[k] = value

    def join_strips():
        def level(k, carry):
            right = pltpu.roll(right_ref[k], 1, axis=1)
            joint_ref[k] = jnp.where(slot == 2, left_ref[k], right)
            return carry

        lax.fori_loop(0, LEVELS, level, 0, unroll=4)

    def gather_edges(x_ref):
        def level(k, carry):
            edge = jnp.zeros((8, LANES), F32)
            for t in range(TILES):
                turned = pltpu.roll(x_ref[k, pl.ds(8 * t + 8, 8), :], 3 * t + 2, axis=1)
                edge = jnp.where(group == t, turned, edge)
            edge_ref[k] = edge
            return carry

        lax.fori_loop(0, LEVELS, level, 0)

    def strip_step():
        _, over, north, south = strip_terms
        for side, ref in ((0, left_ref), (1, right_ref)):
            forward = []
            for k in range(LEVELS):
                x = ref[k]
                up = pltpu.roll(x, 1, axis=1)
                down = pltpu.roll(x, LANES - 1, axis=1)
                if side == 0:
                    down = jnp.where(slot == 2, edge_ref[k], down)
                else:
                    up = jnp.where(slot == 0, pltpu.roll(edge_ref[k], LANES - 1, axis=1), up)
                above = jnp.concatenate([x[1:], pltpu.roll(x, LANES - 3, axis=1)[:1]], 0)
                below = jnp.concatenate([pltpu.roll(x, 3, axis=1)[7:], x[:7]], 0)
                value = over * (up + down) + north * above + south * below
                if k > 0:
                    value = value + strip_ref[side, 0, k - 1] * forward[-1]
                forward.append(value * strip_ref[side, 1, k])
            value = forward[-1]
            ref[LEVELS - 1] = value
            for k in range(LEVELS - 2, -1, -1):
                value = forward[k] + strip_ref[side, 2, k] * value
                ref[k] = value

    def tile_step(t, x_ref, y_ref, out_ref, sums):
        start = pl.multiple_of(8 * t + 8, 8)
        wide = pl.ds(start, 8)
        _, over, north, south = [
            terms_ref[i, pl.ds(pl.multiple_of(8 * t, 8), 8), :] for i in range(4)
        ]
        turn = 126 - 3 * t
        forward = []
        cross = jnp.zeros((8, LANES), F32)
        for k in range(LEVELS):
            x = x_ref[k, wide, :]
            inject = pltpu.roll(joint_ref[k], turn, axis=1)
            west = jnp.where(lane == 0, inject, pltpu.roll(x, 1, axis=1))
            east = jnp.where(lane == LANES - 1, inject, pltpu.roll(x, LANES - 1, axis=1))
            above = x_ref[k, pl.ds(start + 1, 8), :]
            below = x_ref[k, pl.ds(start - 1, 8), :]
            value = over * (west + east) + north * above + south * below
            if sums is not None:
                y_ref[k, pl.ds(pl.multiple_of(8 * t - 8, 8), 8), :] = value
                cross = cross + x * value
            if k > 0:
                value = value + scaled_ref[k - 1, wide, :] * forward[-1]
            forward.append(value * inverse_ref[k, wide, :])
        own = jnp.zeros((8, LANES), F32)
        value = forward[-1]
        for k in range(LEVELS - 1, -1, -1):
            if k < LEVELS - 1:
                value = forward[k] + ratio_ref[k, wide, :] * value
            if out_ref is not None:
                out_ref[k, wide, :] = value
            if sums is not None:
                own = own + value * y_ref[k, pl.ds(pl.multiple_of(8 * t - 8, 8), 8), :]
        if sums is not None:
            return sums[0] + cross, sums[1] + own

    zero = jnp.zeros((8, LANES), F32)

    def start_sum(t, carry):
        wide = pl.ds(pl.multiple_of(8 * t + 8, 8), 8)
        at = pl.ds(pl.multiple_of(8 * t - 8, 8), 8)
        total = zero
        for k in range(LEVELS):
            total = total + x0_ref[k, wide, :] * b_ref[k, at, :]
        return carry + total

    totals = [lax.fori_loop(1, TILES - 1, start_sum, zero)]
    for x_ref, y_ref, out_ref in (
        (x0_ref, y1_ref, x1_ref),
        (x1_ref, y2_ref, x2_ref),
        (x2_ref, y3_ref, None),
    ):
        join_strips()
        totals += lax.fori_loop(
            1,
            TILES - 1,
            lambda t, sums: tile_step(t, x_ref, y_ref, out_ref, sums),
            (zero, zero),
        )
        if out_ref is not None:

            def ends(i, carry):
                tile_step(i * (TILES - 1), x_ref, None, out_ref, None)
                return carry

            lax.fori_loop(0, 2, ends, 0)
            gather_edges(x_ref)
            strip_step()
    sums_ref[...] = jnp.concatenate([jnp.sum(total, axis=0, keepdims=True) for total in totals] + [zero[:1]], 0)


def two_sum(a, b):
    total = a + b
    part = total - a
    return total, (a - (total - part)) + (b - part)


def coefficients(high, low):
    for by in (64, 32, 16, 8, 4, 2, 1):
        high, error = two_sum(high, pltpu.roll(high, by, axis=1))
        low = low + pltpu.roll(low, by, axis=1) + error
    row = lambda x, n: jnp.broadcast_to(x[n : n + 1], (8, LANES))
    shift = jnp.floor(64.0 * (row(high, 1) / row(high, 0)) + 0.5) * (1.0 / 64.0)
    centred = []
    for n in range(7):
        centred.append(row(high, 0) + row(low, 0))
        if n == 6:
            break
        wide = 4097.0 * high
        coarse = wide - (wide - high)
        fine = high - coarse
        following = jnp.concatenate([high[1:], high[:1]], 0)
        rest = jnp.concatenate([low[1:], low[:1]], 0) - shift * low
        total, error = two_sum(following, -shift * coarse)
        rest = rest + error
        total, error = two_sum(total, -shift * fine)
        rest = rest + error
        high = total + rest
        low = rest - (high - total)
    sigma = 1.0 - shift
    energies = [sigma * centred[n] - centred[n + 1] for n in range(6)]
    curvatures = [sigma * energies[n] - energies[n + 1] for n in range(5)]

    def product(p, q, table):
        return sum(p[i] * q[j] * table[i + j] for i in range(len(p)) for j in range(len(q)))

    one = jnp.ones((8, LANES), F32)
    none = jnp.zeros((8, LANES), F32)
    smoothed = [one]
    direction = [one]
    result = []
    energy = energies[0]
    for iteration in range(3):
        length = energy / product(direction, direction, curvatures)
        result = [
            (result[i] if i < len(result) else none) + length * direction[i]
            for i in range(len(direction))
        ]
        if iteration < 2:
            image = [sigma * d for d in direction] + [none]
            image = [image[i] - (direction[i - 1] if i else none) for i in range(len(image))]
            smoothed = [
                (smoothed[i] if i < len(smoothed) else none) - length * image[i]
                for i in range(len(image))
            ]
            following = product(smoothed, smoothed, energies)
            ratio = following / energy
            direction = [
                smoothed[i] + (ratio * direction[i] if i < len(direction) else none)
                for i in range(len(smoothed))
            ]
            energy = following
    k0, k1, k2 = result
    return k0 - shift * k1 + shift * shift * k2, k1 - 2.0 * shift * k2, k2


def last_kernel(
    sums_ref, b_ref, x0_ref, x1_ref, x2_ref, y1_ref, y2_ref, y3_ref, solution_hbm, residual_hbm,
    solution_ref, residual_ref, sems
):
    step = ROWS // CHUNKS
    k0, k1, k2 = coefficients(sums_ref[:8], sums_ref[8:])
    r0, r1, r2 = 1.0 - k0, k0 - k1, k1 - k2

    def copy(i, n):
        src = (solution_ref, residual_ref)[i]
        dst = (solution_hbm, residual_hbm)[i]
        rows = pl.ds(n * step, step)
        return pltpu.make_async_copy(src.at[:, rows, :], dst.at[:, rows, :], sems.at[i, n])

    for n in range(CHUNKS):

        def tile(t, carry):
            at = pl.ds(pl.multiple_of(8 * t - 8, 8), 8)
            wide = pl.ds(pl.multiple_of(8 * t + 8, 8), 8)
            for k in range(LEVELS):
                solution_ref[k, at, :] = (
                    k0 * x0_ref[k, wide, :] + k1 * x1_ref[k, wide, :] + k2 * x2_ref[k, wide, :]
                )
                residual_ref[k, at, :] = (
                    r0 * b_ref[k, at, :] + r1 * y1_ref[k, at, :]
                    + r2 * y2_ref[k, at, :] + k2 * y3_ref[k, at, :]
                )
            return carry

        lax.fori_loop(1 + n * step // 8, 1 + (n + 1) * step // 8, tile, 0)
        for i in range(2):
            copy(i, n).start()
    for n in range(CHUNKS):
        for i in range(2):
            copy(i, n).wait()


VMEM = pl.BlockSpec(memory_space=pltpu.VMEM)
ANY = pl.BlockSpec(memory_space=pl.ANY)


def kept(*shape):
    return pltpu.VMEM(shape, F32)


def call(kernel, outs, ins, in_specs, out_specs=None, scratch=(), limit=24, flops=0, aliases=None):
    return pl.pallas_call(
        kernel,
        out_shape=outs,
        in_specs=in_specs,
        out_specs=[VMEM] * len(outs) if out_specs is None else out_specs,
        scratch_shapes=list(scratch),
        input_output_aliases=aliases or {},
        compiler_params=pltpu.CompilerParams(vmem_limit_bytes=limit * MIB),
        cost_estimate=pl.CostEstimate(flops=flops, bytes_accessed=1000000, transcendentals=0),
        name=kernel.__name__,
    )(*ins)


def total_over_devices(sums):
    high, low = sums, jnp.zeros_like(sums)
    for flip in (1, 2, 66, 4, 12, 16, 48):
        other = swap(jnp.concatenate([high, low], 0), lambda i: i ^ flip)
        high, error = two_sum(high, other[:8])
        low = low + other[8:] + error
    return jnp.concatenate([high, low], 0)


def on_device(right_side, helmholtz, coupling):
    low = pl.BlockSpec((LEVELS, 8, LANES), lambda i: (0, 0, 0))
    high = pl.BlockSpec((LEVELS, 8, LANES), lambda i: (0, ROWS // 8 - 1, 0))
    low_c = pl.BlockSpec((LEVELS - 1, 8, LANES), lambda i: (0, 0, 0))
    high_c = pl.BlockSpec((LEVELS - 1, 8, LANES), lambda i: (0, ROWS // 8 - 1, 0))
    message = jax.ShapeDtypeStruct((STACKED, 8, LANES), F32)
    whole = pl.BlockSpec((STACKED, 8, LANES), lambda i: (0, 0, 0))
    rows_a, rows_b = pl.pallas_call(
        edge_rows_kernel,
        grid=(1,),
        out_shape=[message, message],
        in_specs=[low, high, low, high, low_c, high_c],
        out_specs=[whole, whole],
        name="edge_rows",
    )(right_side, right_side, helmholtz, helmholtz, coupling, coupling)
    rows_a = swap(rows_a, lat_even)
    rows_b = swap(rows_b, lat_odd)
    field = kept(LEVELS, EXTENDED, LANES)
    block = kept(LEVELS, ROWS, LANES)
    b, scaled, inverse, ratio, x0, terms, last, first = call(
        first_kernel,
        [block, field, field, field, field, kept(4, 8 * TILES, LANES)]
        + [kept(STACKED, 8, LANES)] * 2,
        [right_side, helmholtz, coupling],
        [ANY] * 3,
        scratch=[
            pltpu.VMEM((LEVELS, ROWS, LANES), F32),
            pltpu.VMEM((LEVELS - 1, ROWS, LANES), F32),
            pltpu.SemaphoreType.DMA((3, CHUNKS)),
        ],
        flops=10000000,
    )
    south, north, lanes_e, lanes_d = call(
        edge_lanes_kernel,
        [kept(STACKED, 8, LANES)] * 2 + [message, message],
        [rows_a, rows_b, last, first],
        [VMEM] * 4,
    )
    lanes_e = swap(lanes_e, lon_even)
    lanes_d = swap(lanes_d, lon_odd)
    scaled, inverse, ratio, x0, x1, x2, y1, y2, y3, sums = call(
        middle_kernel,
        [field] * 6 + [block] * 3 + [jax.ShapeDtypeStruct((8, LANES), F32)],
        [b, scaled, inverse, ratio, x0, terms, south, north, lanes_e, lanes_d],
        [VMEM] * 10,
        scratch=[
            pltpu.VMEM((LEVELS, 8, LANES), F32),
            pltpu.VMEM((LEVELS, 8, LANES), F32),
            pltpu.VMEM((LEVELS, 8, LANES), F32),
            pltpu.VMEM((LEVELS, 8, LANES), F32),
            pltpu.VMEM((2, 3, LEVELS, 8, LANES), F32),
        ],
        flops=100000000,
        aliases={1: 0, 2: 1, 3: 2, 4: 3},
    )
    sums = total_over_devices(sums)
    result = jax.ShapeDtypeStruct((LEVELS, ROWS, LANES), F32)
    return call(
        last_kernel,
        [result, result],
        [sums, b, x0, x1, x2, y1, y2, y3],
        [VMEM] * 8,
        out_specs=[ANY, ANY],
        scratch=[
            pltpu.VMEM((LEVELS, ROWS, LANES), F32),
            pltpu.VMEM((LEVELS, ROWS, LANES), F32),
            pltpu.SemaphoreType.DMA((2, CHUNKS)),
        ],
        flops=10000000,
    )


def solution(mesh):
    spec = P(None, "lat", "lon")
    return jax.shard_map(
        lambda *args: tuple(on_device(*args)),
        mesh=mesh,
        in_specs=(spec,) * 3,
        out_specs=(spec,) * 2,
        check_vma=False,
    )
```

```python
import functools
import math

import jax
import jax.numpy as jnp
from jax import lax
from jax.experimental import pallas as pl
from jax.experimental.pallas import tpu as pltpu
from jax.sharding import PartitionSpec as P

LEVELS = 20
ROWS = 256
LANES = 128
TOTAL_ROWS = 1024
LON_COEFF = 4.0
TILES = ROWS // 8 + 2
EXTENDED = 8 * TILES + 16
STACKED = 3 * LEVELS - 1
AT_H = LEVELS
AT_C = 2 * LEVELS
CHUNKS = 8
GROUP = 4
PARTIALS = 16
AXES = ("lon", "lat")
F32 = jnp.float32
MIB = 1 << 20


def swap(x, partner):
    return lax.ppermute(x, AXES, [(i, partner(i)) for i in range(128)])


def lat_even(i):
    return i ^ 1


def lat_odd(i):
    lon, lat = i >> 2, i & 3
    if lat in (1, 2):
        return (lon << 2) | (3 - lat)
    return ((lon ^ 16) << 2) | lat


def lon_even(i):
    return i ^ 4


def lon_odd(i):
    lon, lat = i >> 2, i & 3
    other = (lon + 1) % 32 if lon % 2 else (lon - 1) % 32
    return (other << 2) | lat


def lane_index():
    return lax.broadcasted_iota(jnp.int32, (8, LANES), 1)


def sub_index():
    return lax.broadcasted_iota(jnp.int32, (8, LANES), 0)


def capped_cosine(row):
    angle = (row + 0.5) * (math.pi / TOTAL_ROWS) - 0.5 * math.pi
    square = angle * angle
    value = jnp.full_like(row, 0.0)
    for n in range(8, -1, -1):
        value = value * square + (-1.0) ** n / math.factorial(2 * n)
    return jnp.maximum(value, 0.5)


def row_terms(row):
    here = capped_cosine(row)
    return (
        here,
        LON_COEFF / here,
        (here + capped_cosine(row + 1.0)) * 0.5,
        (here + capped_cosine(row - 1.0)) * 0.5,
    )


def eliminate(tiles):
    count = len(tiles)
    below = [None] * count
    ratio = [None] * count
    value = [None] * count
    for k in range(LEVELS):
        for n, (terms, right, helm, coup, store, put, get) in enumerate(tiles):
            cosine, over, north, south = terms
            pivot = cosine * helm(k) + (2.0 * over + north + south)
            scaled = cosine * coup(k) if k < LEVELS - 1 else None
            if scaled is not None:
                pivot = pivot + scaled
            if k > 0:
                pivot = (pivot + below[n]) - below[n] * ratio[n]
            inverse = 1.0 / pivot
            carried = below[n] * inverse if k > 0 else None
            result = right(k) * inverse
            if k > 0:
                result = result + carried * value[n]
            value[n] = result
            put(k, result)
            ratio[n] = scaled * inverse if scaled is not None else None
            below[n] = scaled
            store(k, carried, inverse, ratio[n])
    for k in range(LEVELS - 2, -1, -1):
        for n, (terms, right, helm, coup, store, put, get) in enumerate(tiles):
            value[n] = get(0, k) + get(1, k) * value[n]
            put(k, value[n])


def packed_edges(read, lane):
    last = jnp.zeros((8, LANES), F32)
    first = jnp.zeros((8, LANES), F32)
    group = lane // 3
    for t in range(1, TILES - 1):
        turned = pltpu.roll(read(t), 3 * t + 3, axis=1)
        last = jnp.where(group == t, turned, last)
        first = jnp.where(group == t + 1, turned, first)
    return last, first


def edge_rows_kernel(b_lo, b_hi, h_lo, h_hi, c_lo, c_hi, a_ref, o_ref):
    even = lax.axis_index("lat") % 2 == 0
    for at, count, lo, hi in (
        (0, LEVELS, b_lo, b_hi),
        (AT_H, LEVELS, h_lo, h_hi),
        (AT_C, LEVELS - 1, c_lo, c_hi),
    ):
        low, high = lo[...], hi[...]
        a_ref[pl.ds(at, count)] = jnp.where(even, high, low)
        o_ref[pl.ds(at, count)] = jnp.where(even, low, high)


def pack_kernel(b_hbm, h_hbm, c_hbm, b_ref, h_ref, c_ref, last_ref, first_ref, sems):
    arrays = (
        (b_hbm, b_ref, 0, LEVELS),
        (h_hbm, h_ref, AT_H, LEVELS),
        (c_hbm, c_ref, AT_C, LEVELS - 1),
    )
    parts = []
    for i, (src, dst, at, count) in enumerate(arrays):
        for n in range(CHUNKS):
            lo, hi = count * n // CHUNKS, count * (n + 1) // CHUNKS
            levels = pl.ds(lo, hi - lo)
            copy = pltpu.make_async_copy(src.at[levels], dst.at[levels], sems.at[i, n])
            copy.start()
            parts.append((copy, dst, at, lo, hi))
    lane = lane_index()
    for copy, source, at, lo, hi in parts:
        copy.wait()

        def level(k, carry):
            last, first = packed_edges(lambda t: source[k, pl.ds(8 * t - 8, 8), :], lane)
            last_ref[at + k] = last
            first_ref[at + k] = first
            return carry

        lax.fori_loop(lo, hi, level, 0)


def first_kernel(
    b_ref, h_ref, c_ref, after_ref, carried_ref, inverse_ref, ratio_ref, x_ref, terms_ref, edge_ref,
    sum_ref
):
    del after_ref
    base = lax.axis_index("lat") * ROWS
    lane = lane_index()
    sub = sub_index()

    def row_term(t, carry):
        row = (base + 8 * t - 8 + sub).astype(F32)
        for i, term in enumerate(row_terms(row)):
            terms_ref[i, pl.ds(pl.multiple_of(8 * t, 8), 8), :] = term
        return carry

    lax.fori_loop(0, TILES, row_term, 0, unroll=2)

    def tiles(g, total):
        ats = [pl.ds(pl.multiple_of(32 * g + 8 * n, 8), 8) for n in range(GROUP)]
        wides = [pl.ds(pl.multiple_of(32 * g + 8 * n + 16, 8), 8) for n in range(GROUP)]
        work = []
        for n in range(GROUP):
            at, wide = ats[n], wides[n]
            terms = [
                terms_ref[i, pl.ds(pl.multiple_of(32 * g + 8 * n + 8, 8), 8), :] for i in range(4)
            ]

            def store(k, carried, inverse, ratio, wide=wide):
                inverse_ref[k, wide, :] = inverse
                if carried is not None:
                    carried_ref[k - 1, wide, :] = carried
                if ratio is not None:
                    ratio_ref[k, wide, :] = ratio

            def put(k, value, wide=wide):
                x_ref[k, wide, :] = value

            def get(which, k, wide=wide):
                return (x_ref, ratio_ref)[which][k, wide, :]

            work.append((
                terms,
                lambda k, at=at: b_ref[k, at, :],
                lambda k, at=at: h_ref[k, at, :],
                lambda k, at=at: c_ref[k, at, :],
                store,
                put,
                get,
            ))
        eliminate(work)
        for at, wide in zip(ats, wides):
            for k in range(LEVELS):
                total = total + x_ref[k, wide, :] * b_ref[k, at, :]
        return total

    sum_ref[...] = lax.fori_loop(0, ROWS // 8 // GROUP, tiles, jnp.zeros((8, LANES), F32))
    gather_edges(x_ref, edge_ref, range(1, TILES - 1), lane // 3)


def gather_edges(x_ref, edge_ref, tiles, group, keep=False):
    def level(k, carry):
        edge = edge_ref[k] if keep else jnp.zeros((8, LANES), F32)
        for t in tiles:
            turned = pltpu.roll(x_ref[k, pl.ds(8 * t + 8, 8), :], 3 * t + 2, axis=1)
            edge = jnp.where(group == t, turned, edge)
        edge_ref[k] = edge
        return carry

    lax.fori_loop(0, LEVELS, level, 0, unroll=4 if keep else 1)


def edge_lanes_kernel(a_ref, o_ref, last_ref, first_ref, south_ref, north_ref, e_ref, d_ref):
    lat = lax.axis_index("lat")
    lat_is_even = lat % 2 == 0
    lon_is_even = lax.axis_index("lon") % 2 == 0
    polar = jnp.logical_or(lat == 0, lat == 3)
    lane = lane_index()
    sub = sub_index()
    group = lane // 3

    def level(j, carry):
        near = a_ref[j]
        far = o_ref[j]
        flipped = far
        for s in (0, 1, 2, 5, 6, 7):
            flipped = jnp.where(sub == s, jnp.broadcast_to(far[7 - s : 8 - s], (8, LANES)), flipped)
        far = jnp.where(polar, flipped, far)
        south = jnp.where(lat_is_even, far, near)
        north = jnp.where(lat_is_even, near, far)
        south_ref[j] = south
        north_ref[j] = north
        last, first = last_ref[j], first_ref[j]
        for t, value in ((0, south), (TILES - 1, north)):
            turned = pltpu.roll(value, 3 * t + 3, axis=1)
            last = jnp.where(group == t, turned, last)
            first = jnp.where(group == t + 1, turned, first)
        first = pltpu.roll(first, LANES - 3, axis=1)
        e_ref[j] = jnp.where(lon_is_even, last, first)
        d_ref[j] = jnp.where(lon_is_even, first, last)
        return carry

    for j in range(STACKED):
        level(j, 0)


def middle_kernel(
    carried_in, inverse_in, ratio_in, x0_in, terms_ref, south_ref, north_ref, e_ref, d_ref,
    edge0_ref, sum_ref,
    carried_ref, inverse_ref, ratio_ref, x0_ref, x1_ref, x2_ref, y1_ref, y2_ref, y3_ref, sums_ref,
    left_ref, right_ref, joint_ref, edge_ref, strip_ref
):
    del carried_in, inverse_in, ratio_in, x0_in
    base = lax.axis_index("lat") * ROWS
    lon_is_even = lax.axis_index("lon") % 2 == 0
    lane = lane_index()
    sub = sub_index()
    slot = lane % 3
    group = lane // 3
    strip_terms = row_terms((base + 8 * group - 8 + sub).astype(F32))

    work = []
    for t, source in ((0, south_ref), (TILES - 1, north_ref)):
        wide = pl.ds(8 * t + 8, 8)

        def store(k, carried, inverse, ratio, wide=wide):
            inverse_ref[k, wide, :] = inverse
            if carried is not None:
                carried_ref[k - 1, wide, :] = carried
            if ratio is not None:
                ratio_ref[k, wide, :] = ratio

        def put(k, value, wide=wide):
            x0_ref[k, wide, :] = value

        def get(which, k, wide=wide):
            return (x0_ref, ratio_ref)[which][k, wide, :]

        work.append((
            [terms_ref[i, pl.ds(8 * t, 8), :] for i in range(4)],
            lambda k, source=source: source[k],
            lambda k, source=source: source[AT_H + k],
            lambda k, source=source: source[AT_C + k],
            store,
            put,
            get,
        ))
    for side, out in ((0, left_ref), (1, right_ref)):

        def received(j, side=side):
            even, odd = (d_ref, e_ref) if side == 0 else (e_ref, d_ref)
            return jnp.where(lon_is_even, even[j], odd[j])

        def store(k, carried, inverse, ratio, side=side):
            strip_ref[side, 1, k] = inverse
            if carried is not None:
                strip_ref[side, 0, k] = carried
            if ratio is not None:
                strip_ref[side, 2, k] = ratio

        def put(k, value, out=out):
            out[k] = value

        def get(which, k, side=side, out=out):
            return out[k] if which == 0 else strip_ref[side, 2, k]

        work.append((
            strip_terms,
            received,
            lambda k, received=received: received(AT_H + k),
            lambda k, received=received: received(AT_C + k),
            store,
            put,
            get,
        ))
    eliminate(work)
    for k in range(LEVELS):
        edge = edge0_ref[k]
        for t in (0, TILES - 1):
            turned = pltpu.roll(x0_ref[k, pl.ds(8 * t + 8, 8), :], 3 * t + 2, axis=1)
            edge = jnp.where(group == t, turned, edge)
        edge_ref[k] = edge

    def join_strips():
        for k in range(LEVELS):
            right = pltpu.roll(right_ref[k], 1, axis=1)
            joint_ref[k] = jnp.where(slot == 2, left_ref[k], right)

    def strip_step():
        _, over, north, south = strip_terms
        value = [None, None]
        for k in range(LEVELS):
            for side, ref in ((0, left_ref), (1, right_ref)):
                x = ref[k]
                up = pltpu.roll(x, 1, axis=1)
                down = pltpu.roll(x, LANES - 1, axis=1)
                if side == 0:
                    down = jnp.where(slot == 2, edge_ref[k], down)
                else:
                    up = jnp.where(slot == 0, pltpu.roll(edge_ref[k], LANES - 1, axis=1), up)
                above = jnp.concatenate([x[1:], pltpu.roll(x, LANES - 3, axis=1)[:1]], 0)
                below = jnp.concatenate([pltpu.roll(x, 3, axis=1)[7:], x[:7]], 0)
                y = over * (up + down) + north * above + south * below
                y = y * strip_ref[side, 1, k]
                if k > 0:
                    y = y + strip_ref[side, 0, k] * value[side]
                value[side] = y
                ref[k] = y
        for k in range(LEVELS - 2, -1, -1):
            for side, ref in ((0, left_ref), (1, right_ref)):
                value[side] = ref[k] + strip_ref[side, 2, k] * value[side]
                ref[k] = value[side]

    def step(tiles, x_ref, y_ref, out_ref, sums):
        starts = [pl.multiple_of(8 * t + 8, 8) for t in tiles]
        wides = [pl.ds(start, 8) for start in starts]
        ats = [pl.ds(pl.multiple_of(8 * t - 8, 8), 8) for t in tiles]
        terms = [
            [terms_ref[i, pl.ds(pl.multiple_of(8 * t, 8), 8), :] for i in range(1, 4)] for t in tiles
        ]
        zero = jnp.zeros((8, LANES), F32)
        cross = [zero] * len(tiles)
        own = [zero] * len(tiles)
        forward = [[] for _ in tiles]
        for k in range(LEVELS):
            for n, t in enumerate(tiles):
                over, north, south = terms[n]
                x = x_ref[k, wides[n], :]
                inject = pltpu.roll(joint_ref[k], 126 - 3 * t, axis=1)
                west = jnp.where(lane == 0, inject, pltpu.roll(x, 1, axis=1))
                east = jnp.where(lane == LANES - 1, inject, pltpu.roll(x, LANES - 1, axis=1))
                above = x_ref[k, pl.ds(starts[n] + 1, 8), :]
                below = x_ref[k, pl.ds(starts[n] - 1, 8), :]
                y = over * (west + east) + north * above + south * below
                if sums is not None:
                    y_ref[k, ats[n], :] = y
                    cross[n] = cross[n] + x * y
                y = y * inverse_ref[k, wides[n], :]
                if k > 0:
                    y = y + carried_ref[k - 1, wides[n], :] * forward[n][-1]
                forward[n].append(y)
        value = [f[-1] for f in forward]
        for k in range(LEVELS - 1, -1, -1):
            for n in range(len(tiles)):
                if k < LEVELS - 1:
                    value[n] = forward[n][k] + ratio_ref[k, wides[n], :] * value[n]
                if out_ref is not None:
                    out_ref[k, wides[n], :] = value[n]
                if sums is not None:
                    own[n] = own[n] + value[n] * y_ref[k, ats[n], :]
        if sums is not None:
            return sums[0] + sum(cross), sums[1] + sum(own)

    zero = jnp.zeros((8, LANES), F32)
    totals = [sum_ref[...]]
    for x_ref, y_ref, out_ref in (
        (x0_ref, y1_ref, x1_ref),
        (x1_ref, y2_ref, x2_ref),
        (x2_ref, y3_ref, None),
    ):
        join_strips()
        totals += lax.fori_loop(
            0,
            ROWS // 8 // GROUP,
            lambda g, sums: step(
                [GROUP * g + n + 1 for n in range(GROUP)], x_ref, y_ref, out_ref, sums
            ),
            (zero, zero),
        )
        if out_ref is not None:
            step([0, TILES - 1], x_ref, None, out_ref, None)
            strip_step()
            if x_ref is x0_ref:
                gather_edges(out_ref, edge_ref, range(TILES), group)
    row = zero[:1]
    for n, total in enumerate(totals):
        part = jnp.sum(total, axis=0, keepdims=True)
        for by in (64, 32, 16):
            part = part + pltpu.roll(part, by, axis=1)
        row = jnp.where(lane[:1] // PARTIALS == n, part, row)
    sums_ref[...] = jnp.broadcast_to(row, sums_ref.shape)


def two_sum(a, b):
    total = a + b
    part = total - a
    return total, (a - (total - part)) + (b - part)


def coefficients(parts):
    pairs = [(part, None) for part in parts]
    while len(pairs) > 1:
        joined = []
        for (a, a_low), (b, b_low) in zip(pairs[::2], pairs[1::2]):
            total, error = two_sum(a, b)
            joined.append((total, error if a_low is None else (a_low + b_low) + error))
        pairs = joined
    high, low = pairs[0]
    for axis, by in ((0, 4), (0, 2), (0, 1), (1, 8), (1, 4), (1, 2), (1, 1)):
        by = high.shape[axis] - by
        high, error = two_sum(high, pltpu.roll(high, by, axis=axis))
        low = (low + pltpu.roll(low, by, axis=axis)) + error
    spread = lambda x: jnp.concatenate(
        [jnp.broadcast_to(x[:1, PARTIALS * n : PARTIALS * n + 1], (1, LANES)) for n in range(8)], 0
    )
    high, low = spread(high), spread(low)
    row = lambda x, n: jnp.broadcast_to(x[n : n + 1], (8, LANES))
    shift = jnp.floor(64.0 * (row(high, 1) / row(high, 0)) + 0.5) * (1.0 / 64.0)
    centred = []
    for n in range(7):
        centred.append(row(high, 0) + row(low, 0))
        if n == 6:
            break
        wide = 4097.0 * high
        coarse = wide - (wide - high)
        fine = high - coarse
        following = jnp.concatenate([high[1:], high[:1]], 0)
        rest = jnp.concatenate([low[1:], low[:1]], 0) - shift * low
        total, error = two_sum(following, -shift * coarse)
        rest = rest + error
        total, error = two_sum(total, -shift * fine)
        rest = rest + error
        high = total + rest
        low = rest - (high - total)
    sigma = 1.0 - shift
    energies = [sigma * centred[n] - centred[n + 1] for n in range(6)]
    curvatures = [sigma * energies[n] - energies[n + 1] for n in range(5)]

    def product(p, q, table):
        return sum(p[i] * q[j] * table[i + j] for i in range(len(p)) for j in range(len(q)))

    one = jnp.ones((8, LANES), F32)
    none = jnp.zeros((8, LANES), F32)
    smoothed = [one]
    direction = [one]
    result = []
    energy = energies[0]
    for iteration in range(3):
        length = energy / product(direction, direction, curvatures)
        result = [
            (result[i] if i < len(result) else none) + length * direction[i]
            for i in range(len(direction))
        ]
        if iteration < 2:
            image = [sigma * d for d in direction] + [none]
            image = [image[i] - (direction[i - 1] if i else none) for i in range(len(image))]
            smoothed = [
                (smoothed[i] if i < len(smoothed) else none) - length * image[i]
                for i in range(len(image))
            ]
            following = product(smoothed, smoothed, energies)
            ratio = following / energy
            direction = [
                smoothed[i] + (ratio * direction[i] if i < len(direction) else none)
                for i in range(len(smoothed))
            ]
            energy = following
    k0, k1, k2 = result
    return k0 - shift * k1 + shift * shift * k2, k1 - 2.0 * shift * k2, k2


def last_kernel(
    sums_ref, b_ref, x0_ref, x1_ref, x2_ref, y1_ref, y2_ref, y3_ref, solution_hbm, residual_hbm,
    solution_ref, residual_ref, sems
):
    step = ROWS // CHUNKS
    k0, k1, k2 = coefficients([sums_ref[8 * n : 8 * n + 8] for n in range(16)])
    r0, r1, r2 = 1.0 - k0, k0 - k1, k1 - k2

    def copy(i, n):
        src = (solution_ref, residual_ref)[i]
        dst = (solution_hbm, residual_hbm)[i]
        rows = pl.ds(n * step, step)
        return pltpu.make_async_copy(src.at[:, rows, :], dst.at[:, rows, :], sems.at[i, n])

    for n in range(CHUNKS):

        def tile(t, carry):
            at = pl.ds(pl.multiple_of(8 * t - 8, 8), 8)
            wide = pl.ds(pl.multiple_of(8 * t + 8, 8), 8)
            for k in range(LEVELS):
                solution_ref[k, at, :] = (
                    k0 * x0_ref[k, wide, :] + k1 * x1_ref[k, wide, :] + k2 * x2_ref[k, wide, :]
                )
                residual_ref[k, at, :] = (
                    r0 * b_ref[k, at, :] + r1 * y1_ref[k, at, :]
                    + r2 * y2_ref[k, at, :] + k2 * y3_ref[k, at, :]
                )
            return carry

        lax.fori_loop(1 + n * step // 8, 1 + (n + 1) * step // 8, tile, 0)
        for i in range(2):
            copy(i, n).start()
    for n in range(CHUNKS):
        for i in range(2):
            copy(i, n).wait()


VMEM = pl.BlockSpec(memory_space=pltpu.VMEM)
ANY = pl.BlockSpec(memory_space=pl.ANY)
HBM = pl.BlockSpec(memory_space=pltpu.HBM)


def kept(*shape):
    return pltpu.VMEM(shape, F32)


def call(kernel, outs, ins, in_specs, out_specs=None, scratch=(), limit=8, flops=0, aliases=None):
    return pl.pallas_call(
        kernel,
        out_shape=outs,
        in_specs=in_specs,
        out_specs=[VMEM] * len(outs) if out_specs is None else out_specs,
        scratch_shapes=list(scratch),
        input_output_aliases=aliases or {},
        compiler_params=pltpu.CompilerParams(vmem_limit_bytes=limit * MIB),
        cost_estimate=pl.CostEstimate(flops=flops, bytes_accessed=1000000, transcendentals=0),
        name=kernel.__name__,
    )(*ins)


def on_device(right_side, helmholtz, coupling):
    right_side, helmholtz, coupling = [
        pltpu.with_memory_space_constraint(x, pltpu.HBM) for x in (right_side, helmholtz, coupling)
    ]
    low = pl.BlockSpec((LEVELS, 8, LANES), lambda i: (0, 0, 0))
    high = pl.BlockSpec((LEVELS, 8, LANES), lambda i: (0, ROWS // 8 - 1, 0))
    low_c = pl.BlockSpec((LEVELS - 1, 8, LANES), lambda i: (0, 0, 0))
    high_c = pl.BlockSpec((LEVELS - 1, 8, LANES), lambda i: (0, ROWS // 8 - 1, 0))
    message = jax.ShapeDtypeStruct((STACKED, 8, LANES), F32)
    whole = pl.BlockSpec((STACKED, 8, LANES), lambda i: (0, 0, 0))
    rows_a, rows_b = pl.pallas_call(
        edge_rows_kernel,
        grid=(1,),
        out_shape=[message, message],
        in_specs=[low, high, low, high, low_c, high_c],
        out_specs=[whole, whole],
        name="edge_rows",
    )(right_side, right_side, helmholtz, helmholtz, coupling, coupling)
    rows_a = swap(rows_a, lat_even)
    rows_b = swap(rows_b, lat_odd)
    field = kept(LEVELS, EXTENDED, LANES)
    block = kept(LEVELS, ROWS, LANES)
    stack = kept(STACKED, 8, LANES)
    edges = kept(LEVELS, 8, LANES)
    b, h, c, last, first = call(
        pack_kernel,
        [block, block, kept(LEVELS - 1, ROWS, LANES), stack, stack],
        [right_side, helmholtz, coupling],
        [HBM] * 3,
        scratch=[pltpu.SemaphoreType.DMA((3, CHUNKS))],
        flops=10000000,
    )
    south, north, lanes_e, lanes_d = call(
        edge_lanes_kernel,
        [stack, stack, message, message],
        [rows_a, rows_b, last, first],
        [VMEM] * 4,
    )
    carried, inverse, ratio, x0, terms, edge0, sum0 = call(
        first_kernel,
        [field] * 4 + [kept(4, 8 * TILES, LANES), edges, kept(8, LANES)],
        [b, h, c, lanes_d],
        [VMEM] * 3 + [ANY],
        flops=10000000,
    )
    lanes_e = swap(lanes_e, lon_even)
    lanes_d = swap(lanes_d, lon_odd)
    carried, inverse, ratio, x0, x1, x2, y1, y2, y3, sums = call(
        middle_kernel,
        [field] * 6 + [block] * 3 + [jax.ShapeDtypeStruct((128, LANES), F32)],
        [carried, inverse, ratio, x0, terms, south, north, lanes_e, lanes_d, edge0, sum0],
        [VMEM] * 11,
        scratch=[
            pltpu.VMEM((LEVELS, 8, LANES), F32),
            pltpu.VMEM((LEVELS, 8, LANES), F32),
            pltpu.VMEM((LEVELS, 8, LANES), F32),
            pltpu.VMEM((LEVELS, 8, LANES), F32),
            pltpu.VMEM((2, 3, LEVELS, 8, LANES), F32),
        ],
        flops=100000000,
        aliases={0: 0, 1: 1, 2: 2, 3: 3},
    )
    sums = lax.all_to_all(sums, AXES, 0, 0, tiled=True)
    result = jax.ShapeDtypeStruct((LEVELS, ROWS, LANES), F32)
    return call(
        last_kernel,
        [result, result],
        [sums, b, x0, x1, x2, y1, y2, y3],
        [VMEM] * 8,
        out_specs=[ANY, ANY],
        scratch=[
            pltpu.VMEM((LEVELS, ROWS, LANES), F32),
            pltpu.VMEM((LEVELS, ROWS, LANES), F32),
            pltpu.SemaphoreType.DMA((2, CHUNKS)),
        ],
        flops=10000000,
    )


def solution(mesh):
    spec = P(None, "lat", "lon")
    return jax.shard_map(
        lambda *args: tuple(on_device(*args)),
        mesh=mesh,
        in_specs=(spec,) * 3,
        out_specs=(spec,) * 2,
        check_vma=False,
    )
```

```python
import functools
import math

import jax
import jax.numpy as jnp
from jax import lax
from jax.experimental import pallas as pl
from jax.experimental.pallas import tpu as pltpu
from jax.sharding import PartitionSpec as P

LEVELS = 20
ROWS = 256
LANES = 128
TOTAL_ROWS = 1024
LON_COEFF = 4.0
TILES = ROWS // 8 + 2
EXTENDED = 8 * TILES + 16
STACKED = 3 * LEVELS - 1
AT_H = LEVELS
AT_C = 2 * LEVELS
CHUNKS = 8
GROUP = 8
PARTIALS = 16
PAD = 8
LANE_MESSAGE = LEVELS + (2 * LEVELS + 1) // 3
AXES = ("lon", "lat")
F32 = jnp.float32
MIB = 1 << 20


def swap(x, partner):
    return lax.ppermute(x, AXES, [(i, partner(i)) for i in range(128)])


def lat_even(i):
    return i ^ 1


def lat_odd(i):
    lon, lat = i >> 2, i & 3
    if lat in (1, 2):
        return (lon << 2) | (3 - lat)
    return ((lon ^ 16) << 2) | lat


def lon_even(i):
    return i ^ 4


def lon_odd(i):
    lon, lat = i >> 2, i & 3
    other = (lon + 1) % 32 if lon % 2 else (lon - 1) % 32
    return (other << 2) | lat


def lane_index():
    return lax.broadcasted_iota(jnp.int32, (8, LANES), 1)


def sub_index():
    return lax.broadcasted_iota(jnp.int32, (8, LANES), 0)


def capped_cosine(row):
    angle = (row + 0.5) * (math.pi / TOTAL_ROWS) - 0.5 * math.pi
    square = angle * angle
    value = jnp.full_like(row, 0.0)
    for n in range(8, -1, -1):
        value = value * square + (-1.0) ** n / math.factorial(2 * n)
    return jnp.maximum(value, 0.5)


def row_terms(row):
    here = capped_cosine(row)
    return (
        here,
        LON_COEFF / here,
        (here + capped_cosine(row + 1.0)) * 0.5,
        (here + capped_cosine(row - 1.0)) * 0.5,
    )


def eliminate(tiles):
    count = len(tiles)
    below = [None] * count
    ratio = [None] * count
    value = [None] * count
    total = [None] * count
    for k in range(LEVELS):
        for n, (terms, right, helm, coup, store, put, get) in enumerate(tiles):
            cosine, over, north, south = terms
            pivot = cosine * helm(k) + (2.0 * over + north + south)
            scaled = cosine * coup(k) if k < LEVELS - 1 else None
            if scaled is not None:
                pivot = pivot + scaled
            if k > 0:
                pivot = (pivot + below[n]) - below[n] * ratio[n]
            inverse = 1.0 / pivot
            summed = right(k)
            if k > 0:
                summed = summed + below[n] * value[n]
            value[n] = summed * inverse
            total[n] = summed * value[n] if k == 0 else total[n] + summed * value[n]
            put(k, value[n])
            ratio[n] = scaled * inverse if scaled is not None else None
            below[n] = scaled
            store(k, scaled, inverse, ratio[n])
    for k in range(LEVELS - 2, -1, -1):
        for n, (terms, right, helm, coup, store, put, get) in enumerate(tiles):
            value[n] = get(0, k) + get(1, k) * value[n]
            put(k, value[n])
    return total


def rows_beside(x):
    above = jnp.concatenate([x[1:], pltpu.roll(x, LANES - 3, axis=1)[:1]], 0)
    below = jnp.concatenate([pltpu.roll(x, 3, axis=1)[7:], x[:7]], 0)
    return above, below


def packed_edges(read, lane):
    last = jnp.zeros((8, LANES), F32)
    first = jnp.zeros((8, LANES), F32)
    group = lane // 3
    for t in range(1, TILES - 1):
        turned = pltpu.roll(read(t), 3 * t + 3, axis=1)
        last = jnp.where(group == t, turned, last)
        first = jnp.where(group == t + 1, turned, first)
    return last, first


def edge_rows_kernel(b_lo, b_hi, h_lo, h_hi, c_lo, c_hi, a_ref, o_ref):
    lat = lax.axis_index("lat")
    even = lat % 2 == 0
    levels = [
        (at + k, lo, hi, k)
        for at, count, lo, hi in (
            (0, LEVELS, b_lo, b_hi),
            (AT_H, LEVELS, h_lo, h_hi),
            (AT_C, LEVELS - 1, c_lo, c_hi),
        )
        for k in range(count)
    ]

    def put_high(ref):
        for j, lo, hi, k in reversed(levels):
            ref[pl.ds(PAD + 3 * j - 5, 8), :] = hi[k]

    def put_low(ref):
        for j, lo, hi, k in levels:
            ref[pl.ds(PAD + 3 * j, 8), :] = lo[k]

    @pl.when(even)
    def _():
        put_high(a_ref)

    @pl.when(jnp.logical_not(even))
    def _():
        put_low(a_ref)

    @pl.when(lat == 0)
    def _():
        for j, lo, hi, k in levels:
            for i in range(3):
                o_ref[pl.ds(PAD + 3 * j + i, 1), :] = lo[k, pl.ds(2 - i, 1), :]

    @pl.when(lat == 1)
    def _():
        put_high(o_ref)

    @pl.when(lat == 2)
    def _():
        put_low(o_ref)

    @pl.when(lat == 3)
    def _():
        for j, lo, hi, k in levels:
            for i in range(3):
                o_ref[pl.ds(PAD + 3 * j + i, 1), :] = hi[k, pl.ds(7 - i, 1), :]


def pack_kernel(b_hbm, h_hbm, c_hbm, b_ref, h_ref, c_ref, last_ref, first_ref, sems):
    arrays = (
        (b_hbm, b_ref, 0, LEVELS),
        (h_hbm, h_ref, AT_H, LEVELS),
        (c_hbm, c_ref, AT_C, LEVELS - 1),
    )
    parts = []
    for i, (src, dst, at, count) in enumerate(arrays):
        for n in range(CHUNKS):
            lo, hi = count * n // CHUNKS, count * (n + 1) // CHUNKS
            levels = pl.ds(lo, hi - lo)
            copy = pltpu.make_async_copy(src.at[levels], dst.at[levels], sems.at[i, n])
            copy.start()
            parts.append((copy, dst, at, lo, hi))
    lane = lane_index()
    for copy, source, at, lo, hi in parts:
        copy.wait()

        for k in range(lo, hi):
            last, first = packed_edges(lambda t: source[k, pl.ds(8 * t - 8, 8), :], lane)
            last_ref[at + k] = last
            first_ref[at + k] = first


def first_kernel(
    b_ref, h_ref, c_ref, halo_ref, scaled_ref, inverse_ref, ratio_ref, x_ref, terms_ref, edge_ref,
    sum_ref, y_ref
):
    base = lax.axis_index("lat") * ROWS
    lane = lane_index()
    sub = sub_index()

    def row_term(t, carry):
        row = (base + 8 * t - 8 + sub).astype(F32)
        for i, term in enumerate(row_terms(row)):
            terms_ref[i, pl.ds(pl.multiple_of(8 * t, 8), 8), :] = term
        return carry

    lax.fori_loop(0, TILES, row_term, 0, unroll=2)
    for n, t in ((0, 0), (1, TILES - 1)):
        for k in range(LEVELS):
            wide = pl.ds(8 * t + 8, 8)
            x_ref[k, wide, :] = halo_ref[n, 0, k]
            inverse_ref[k, wide, :] = halo_ref[n, 2, k]
            if k < LEVELS - 1:
                scaled_ref[k, wide, :] = halo_ref[n, 1, k]
                ratio_ref[k, wide, :] = halo_ref[n, 3, k]

    def tiles(g, total):
        work = []
        for n in range(4):
            at = pl.ds(pl.multiple_of(32 * g + 8 * n, 8), 8)
            wide = pl.ds(pl.multiple_of(32 * g + 8 * n + 16, 8), 8)
            terms = [
                terms_ref[i, pl.ds(pl.multiple_of(32 * g + 8 * n + 8, 8), 8), :] for i in range(4)
            ]

            def store(k, scaled, inverse, ratio, wide=wide):
                inverse_ref[k, wide, :] = inverse
                if scaled is not None:
                    scaled_ref[k, wide, :] = scaled
                    ratio_ref[k, wide, :] = ratio

            def put(k, value, wide=wide):
                x_ref[k, wide, :] = value

            def get(which, k, wide=wide):
                return (x_ref, ratio_ref)[which][k, wide, :]

            work.append((
                terms,
                lambda k, at=at: b_ref[k, at, :],
                lambda k, at=at: h_ref[k, at, :],
                lambda k, at=at: c_ref[k, at, :],
                store,
                put,
                get,
            ))
        return total + sum(eliminate(work))

    sum_ref[...] = lax.fori_loop(0, ROWS // 32, tiles, jnp.zeros((8, LANES), F32))
    gather_edges(x_ref, edge_ref, range(TILES), lane // 3)

    def neighbours(g, carry):
        for n in range(4):
            start = pl.multiple_of(32 * g + 8 * n + 16, 8)
            here = pl.ds(pl.multiple_of(32 * g + 8 * n + 8, 8), 8)
            over, north, south = [terms_ref[i, here, :] for i in range(1, 4)]
            for k in range(LEVELS):
                x = x_ref[k, pl.ds(start, 8), :]
                west = jnp.where(lane == 0, 0.0, pltpu.roll(x, 1, axis=1))
                east = jnp.where(lane == LANES - 1, 0.0, pltpu.roll(x, LANES - 1, axis=1))
                above = x_ref[k, pl.ds(start + 1, 8), :]
                below = x_ref[k, pl.ds(start - 1, 8), :]
                y_ref[k, pl.ds(pl.multiple_of(32 * g + 8 * n, 8), 8), :] = (
                    over * (west + east) + north * above + south * below
                )
        return carry

    lax.fori_loop(0, ROWS // 32, neighbours, 0)


def gather_edges(x_ref, edge_ref, tiles, group):
    def level(k, carry):
        edge = jnp.zeros((8, LANES), F32)
        for t in tiles:
            turned = pltpu.roll(x_ref[k, pl.ds(8 * t + 8, 8), :], 3 * t + 2, axis=1)
            edge = jnp.where(group == t, turned, edge)
        edge_ref[k] = edge
        return carry

    lax.fori_loop(0, LEVELS, level, 0, unroll=2)


def edge_lanes_kernel(
    a_ref, o_ref, last_ref, first_ref, halo_ref, e_ref, d_ref, raw_ref, strip_ref, part_ref
):
    even = lax.axis_index("lat") % 2 == 0
    lon_is_even = lax.axis_index("lon") % 2 == 0
    base = lax.axis_index("lat") * ROWS
    lane = lane_index()
    sub = sub_index()
    group = lane // 3
    slot = lane % 3
    for j in range(STACKED):
        low, high = pl.ds(PAD + 3 * j - 5, 8), pl.ds(PAD + 3 * j, 8)
        south = jnp.where(even, o_ref[low, :], a_ref[low, :])
        north = jnp.where(even, a_ref[high, :], o_ref[high, :])
        raw_ref[0, j] = south
        raw_ref[1, j] = north
        last, first = last_ref[j], first_ref[j]
        for t, value in ((0, south), (TILES - 1, north)):
            turned = pltpu.roll(value, 3 * t + 3, axis=1)
            last = jnp.where(group == t, turned, last)
            first = jnp.where(group == t + 1, turned, first)
        raw_ref[2, j] = last
        raw_ref[3, j] = pltpu.roll(first, LANES - 3, axis=1)
    strip_terms = row_terms((base + 8 * group - 8 + sub).astype(F32))
    work = []
    for n in range(4):
        if n < 2:
            terms = row_terms((base + (TILES - 1) * 8 * n - 8 + sub).astype(F32))
            keep = halo_ref.at[n]
        else:
            terms = strip_terms
            keep = strip_ref.at[n - 2]

        def store(k, scaled, inverse, ratio, keep=keep):
            keep[2, k] = inverse
            if scaled is not None:
                keep[1, k] = scaled
                keep[3, k] = ratio

        def put(k, value, keep=keep):
            keep[0, k] = value

        def get(which, k, keep=keep):
            return keep[3 * which, k]

        work.append((
            terms,
            lambda k, n=n: raw_ref[n, k],
            lambda k, n=n: raw_ref[n, AT_H + k],
            lambda k, n=n: raw_ref[n, AT_C + k],
            store,
            put,
            get,
        ))
    eliminate(work)
    _, over, north, south = strip_terms
    value = [None, None]
    for k in range(LEVELS):
        for side in (0, 1):
            x = strip_ref[side, 0, k]
            up = pltpu.roll(x, 1, axis=1)
            down = pltpu.roll(x, LANES - 1, axis=1)
            if side == 0:
                down = jnp.where(slot == 2, 0.0, down)
            else:
                up = jnp.where(slot == 0, 0.0, up)
            above, below = rows_beside(x)
            y = over * (up + down) + north * above + south * below
            part_ref[side, 0, k] = y
            if k > 0:
                y = y + strip_ref[side, 1, k - 1] * value[side]
            value[side] = y * strip_ref[side, 2, k]
            part_ref[side, 1, k] = value[side]
    for k in range(LEVELS - 1, -1, -1):
        messages = []
        for side in (0, 1):
            if k < LEVELS - 1:
                value[side] = part_ref[side, 1, k] + strip_ref[side, 3, k] * value[side]
            outer = 2 - 2 * side
            known = pltpu.roll(part_ref[side, 0, k], (2 - 2 * outer) % LANES, axis=1)
            message = jnp.where(slot == outer, strip_ref[side, 0, k], known)
            messages.append(jnp.where(slot == 1, value[side], message))
        last, first = messages
        e_ref[k] = jnp.where(lon_is_even, last, first)
        d_ref[k] = jnp.where(lon_is_even, first, last)
    for m in range(LEVELS, LANE_MESSAGE):
        messages = []
        for side in (0, 1):
            outer = 2 - 2 * side
            message = jnp.zeros((8, LANES), F32)
            for q in range(3):
                at = 3 * (m - LEVELS) + q
                source = strip_ref[side, 2, at] if at < LEVELS else strip_ref[side, 1, at - LEVELS]
                message = jnp.where(slot == q, pltpu.roll(source, (q - outer) % LANES, axis=1), message)
            messages.append(message)
        last, first = messages
        e_ref[m] = jnp.where(lon_is_even, last, first)
        d_ref[m] = jnp.where(lon_is_even, first, last)


def middle_kernel(
    scaled_ref, inverse_ref, ratio_ref, x0_ref, y1_in, terms_ref, e_ref, d_ref, edge0_ref, sum_ref,
    y1_ref, x1_ref, x2_ref, y2_ref, y3_ref, sums_ref, strip0_ref, strip_ref, further_ref, edge_ref,
    factor_ref
):
    del y1_in
    base = lax.axis_index("lat") * ROWS
    lon_is_even = lax.axis_index("lon") % 2 == 0
    lane = lane_index()
    sub = sub_index()
    slot = lane % 3
    group = lane // 3
    _, strip_over, strip_north, strip_south = row_terms((base + 8 * group - 8 + sub).astype(F32))

    def turned(x, by):
        return pltpu.roll(x, by % LANES, axis=1) if by % LANES else x

    def arrived(m):
        e, d = e_ref[m], d_ref[m]
        return jnp.where(lon_is_even, d, e), jnp.where(lon_is_even, e, d)

    for m in range(LEVELS, LANE_MESSAGE):
        left, right = arrived(m)
        for q in range(3):
            at = 3 * (m - LEVELS) + q
            value = jnp.where(slot == 2, turned(left, 2 - q), turned(right, 1 - q))
            if at < LEVELS:
                factor_ref[1, at] = value
            else:
                factor_ref[0, at - LEVELS] = value
    for k in range(LEVELS - 1):
        factor_ref[2, k] = factor_ref[0, k] * factor_ref[1, k]

    def solve_strip(right, out_ref):
        value = None
        for k in range(LEVELS):
            y = right(k)
            if k > 0:
                y = y + factor_ref[0, k - 1] * value
            value = y * factor_ref[1, k]
            out_ref[k] = value
        for k in range(LEVELS - 2, -1, -1):
            value = out_ref[k] + factor_ref[2, k] * value
            out_ref[k] = value

    def first_right(k):
        left, right = arrived(k)
        strip0_ref[k] = jnp.where(slot == 2, left, turned(right, 1))
        further_ref[k] = jnp.where(slot == 2, turned(left, 1), right)
        known = jnp.where(slot == 2, turned(left, 2), turned(right, -1))
        return known + strip_over * edge0_ref[k]

    def second_right(k):
        above, below = rows_beside(strip_ref[k])
        beside = further_ref[k] + edge_ref[k]
        return strip_over * beside + strip_north * above + strip_south * below

    def step(tiles, x_ref, y_ref, out_ref, halo_ref, sums, begun=False):
        starts = [pl.multiple_of(8 * t + 8, 8) for t in tiles]
        wides = [pl.ds(start, 8) for start in starts]
        ats = [pl.ds(pl.multiple_of(8 * t - 8, 8), 8) for t in tiles]
        terms = [
            [terms_ref[i, pl.ds(pl.multiple_of(8 * t, 8), 8), :] for i in range(1, 4)] for t in tiles
        ]
        zero = jnp.zeros((8, LANES), F32)
        cross = [zero] * len(tiles)
        own = [zero] * len(tiles)
        forward = [[] for _ in tiles]
        for k in range(LEVELS):
            for n, t in enumerate(tiles):
                over, north, south = terms[n]
                x = x_ref[k, wides[n], :]
                inject = pltpu.roll(halo_ref[k], 126 - 3 * t, axis=1)
                if begun:
                    inject = jnp.where((lane == 0) | (lane == LANES - 1), inject, 0.0)
                    y = y_ref[k, ats[n], :] + over * inject
                else:
                    west = jnp.where(lane == 0, inject, pltpu.roll(x, 1, axis=1))
                    east = jnp.where(lane == LANES - 1, inject, pltpu.roll(x, LANES - 1, axis=1))
                    above = x_ref[k, pl.ds(starts[n] + 1, 8), :]
                    below = x_ref[k, pl.ds(starts[n] - 1, 8), :]
                    y = over * (west + east) + north * above + south * below
                if sums is not None:
                    y_ref[k, ats[n], :] = y
                    cross[n] = cross[n] + x * y
                if k > 0:
                    y = y + scaled_ref[k - 1, wides[n], :] * forward[n][-1]
                value = y * inverse_ref[k, wides[n], :]
                if sums is not None:
                    own[n] = own[n] + y * value
                forward[n].append(value)
        if out_ref is not None:
            value = [f[-1] for f in forward]
            for k in range(LEVELS - 1, -1, -1):
                for n in range(len(tiles)):
                    if k < LEVELS - 1:
                        value[n] = forward[n][k] + ratio_ref[k, wides[n], :] * value[n]
                    out_ref[k, wides[n], :] = value[n]
        if sums is not None:
            return sums[0] + sum(cross), sums[1] + sum(own)

    zero = jnp.zeros((8, LANES), F32)
    totals = [sum_ref[...]]
    solve_strip(first_right, strip_ref)
    for x_ref, y_ref, out_ref, halo_ref in (
        (x0_ref, y1_ref, x1_ref, strip0_ref),
        (x1_ref, y2_ref, x2_ref, strip_ref),
        (x2_ref, y3_ref, None, strip_ref),
    ):
        totals += lax.fori_loop(
            0,
            ROWS // 8 // GROUP,
            lambda g, sums: step(
                [GROUP * g + n + 1 for n in range(GROUP)], x_ref, y_ref, out_ref, halo_ref, sums,
                x_ref is x0_ref
            ),
            (zero, zero),
        )
        if out_ref is not None:
            step([0, TILES - 1], x_ref, None, out_ref, halo_ref, None)
        if x_ref is x0_ref:
            gather_edges(out_ref, edge_ref, range(TILES), group)
        elif x_ref is x1_ref:
            solve_strip(second_right, strip_ref)
    row = zero[:1]
    for n, total in enumerate(totals):
        part = jnp.sum(total, axis=0, keepdims=True)
        for by in (64, 32, 16):
            part = part + pltpu.roll(part, by, axis=1)
        row = jnp.where(lane[:1] // PARTIALS == n, part, row)
    sums_ref[...] = jnp.broadcast_to(row, sums_ref.shape)


def two_sum(a, b):
    total = a + b
    part = total - a
    return total, (a - (total - part)) + (b - part)


def coefficients(parts):
    pairs = [(part, None) for part in parts]
    while len(pairs) > 1:
        joined = []
        for (a, a_low), (b, b_low) in zip(pairs[::2], pairs[1::2]):
            total, error = two_sum(a, b)
            joined.append((total, error if a_low is None else (a_low + b_low) + error))
        pairs = joined
    high, low = pairs[0]
    for axis, by in ((0, 4), (0, 2), (0, 1), (1, 8), (1, 4), (1, 2), (1, 1)):
        by = high.shape[axis] - by
        high, error = two_sum(high, pltpu.roll(high, by, axis=axis))
        low = (low + pltpu.roll(low, by, axis=axis)) + error
    spread = lambda x: jnp.concatenate(
        [jnp.broadcast_to(x[:1, PARTIALS * n : PARTIALS * n + 1], (1, LANES)) for n in range(8)], 0
    )
    high, low = spread(high), spread(low)
    row = lambda x, n: jnp.broadcast_to(x[n : n + 1], (8, LANES))
    shift = jnp.floor(64.0 * (row(high, 1) / row(high, 0)) + 0.5) * (1.0 / 64.0)
    centred = []
    for n in range(7):
        centred.append(row(high, 0) + row(low, 0))
        if n == 6:
            break
        wide = 4097.0 * high
        coarse = wide - (wide - high)
        fine = high - coarse
        following = jnp.concatenate([high[1:], high[:1]], 0)
        rest = jnp.concatenate([low[1:], low[:1]], 0) - shift * low
        total, error = two_sum(following, -shift * coarse)
        rest = rest + error
        total, error = two_sum(total, -shift * fine)
        rest = rest + error
        high = total + rest
        low = rest - (high - total)
    sigma = 1.0 - shift
    energies = [sigma * centred[n] - centred[n + 1] for n in range(6)]
    curvatures = [sigma * energies[n] - energies[n + 1] for n in range(5)]

    def product(p, q, table):
        return sum(p[i] * q[j] * table[i + j] for i in range(len(p)) for j in range(len(q)))

    one = jnp.ones((8, LANES), F32)
    none = jnp.zeros((8, LANES), F32)
    smoothed = [one]
    direction = [one]
    result = []
    energy = energies[0]
    for iteration in range(3):
        length = energy / product(direction, direction, curvatures)
        result = [
            (result[i] if i < len(result) else none) + length * direction[i]
            for i in range(len(direction))
        ]
        if iteration < 2:
            image = [sigma * d for d in direction] + [none]
            image = [image[i] - (direction[i - 1] if i else none) for i in range(len(image))]
            smoothed = [
                (smoothed[i] if i < len(smoothed) else none) - length * image[i]
                for i in range(len(image))
            ]
            following = product(smoothed, smoothed, energies)
            ratio = following / energy
            direction = [
                smoothed[i] + (ratio * direction[i] if i < len(direction) else none)
                for i in range(len(smoothed))
            ]
            energy = following
    k0, k1, k2 = result
    return k0 - shift * k1 + shift * shift * k2, k1 - 2.0 * shift * k2, k2


def last_kernel(
    sums_ref, b_ref, x0_ref, x1_ref, x2_ref, y1_ref, y2_ref, y3_ref, solution_hbm, residual_hbm,
    solution_ref, residual_ref, sems
):
    step = ROWS // CHUNKS
    k0, k1, k2 = coefficients([sums_ref[8 * n : 8 * n + 8] for n in range(16)])
    r0, r1, r2 = 1.0 - k0, k0 - k1, k1 - k2

    def copy(i, n):
        src = (solution_ref, residual_ref)[i]
        dst = (solution_hbm, residual_hbm)[i]
        rows = pl.ds(n * step, step)
        return pltpu.make_async_copy(src.at[:, rows, :], dst.at[:, rows, :], sems.at[i, n])

    for n in range(CHUNKS):

        def tile(t, carry):
            at = pl.ds(pl.multiple_of(8 * t - 8, 8), 8)
            wide = pl.ds(pl.multiple_of(8 * t + 8, 8), 8)
            for k in range(LEVELS):
                solution_ref[k, at, :] = (
                    k0 * x0_ref[k, wide, :] + k1 * x1_ref[k, wide, :] + k2 * x2_ref[k, wide, :]
                )
                residual_ref[k, at, :] = (
                    r0 * b_ref[k, at, :] + r1 * y1_ref[k, at, :]
                    + r2 * y2_ref[k, at, :] + k2 * y3_ref[k, at, :]
                )
            return carry

        lax.fori_loop(1 + n * step // 8, 1 + (n + 1) * step // 8, tile, 0)
        for i in range(2):
            copy(i, n).start()
    for n in range(CHUNKS):
        for i in range(2):
            copy(i, n).wait()


VMEM = pl.BlockSpec(memory_space=pltpu.VMEM)
ANY = pl.BlockSpec(memory_space=pl.ANY)
HBM = pl.BlockSpec(memory_space=pltpu.HBM)


def kept(*shape):
    return pltpu.VMEM(shape, F32)


def call(kernel, outs, ins, in_specs, out_specs=None, scratch=(), limit=8, flops=0, aliases=None):
    return pl.pallas_call(
        kernel,
        out_shape=outs,
        in_specs=in_specs,
        out_specs=[VMEM] * len(outs) if out_specs is None else out_specs,
        scratch_shapes=list(scratch),
        input_output_aliases=aliases or {},
        compiler_params=pltpu.CompilerParams(vmem_limit_bytes=limit * MIB),
        cost_estimate=pl.CostEstimate(flops=flops, bytes_accessed=1000000, transcendentals=0),
        name=kernel.__name__,
    )(*ins)


def on_device(right_side, helmholtz, coupling):
    right_side, helmholtz, coupling = [
        pltpu.with_memory_space_constraint(x, pltpu.HBM) for x in (right_side, helmholtz, coupling)
    ]
    low = pl.BlockSpec((LEVELS, 8, LANES), lambda i: (0, 0, 0))
    high = pl.BlockSpec((LEVELS, 8, LANES), lambda i: (0, ROWS // 8 - 1, 0))
    low_c = pl.BlockSpec((LEVELS - 1, 8, LANES), lambda i: (0, 0, 0))
    high_c = pl.BlockSpec((LEVELS - 1, 8, LANES), lambda i: (0, ROWS // 8 - 1, 0))
    message_rows = -(-(PAD + 3 * STACKED + 5) // 8) * 8
    rows_a, rows_b = pl.pallas_call(
        edge_rows_kernel,
        grid=(1,),
        out_shape=[kept(message_rows, LANES)] * 2,
        in_specs=[low, high, low, high, low_c, high_c],
        out_specs=[pl.BlockSpec((message_rows, LANES), lambda i: (0, 0))] * 2,
        name="edge_rows",
    )(right_side, right_side, helmholtz, helmholtz, coupling, coupling)
    rows_a = swap(rows_a, lat_even)
    rows_b = swap(rows_b, lat_odd)
    field = kept(LEVELS, EXTENDED, LANES)
    block = kept(LEVELS, ROWS, LANES)
    stack = kept(STACKED, 8, LANES)
    edges = kept(LEVELS, 8, LANES)
    message = kept(LANE_MESSAGE, 8, LANES)
    tile_scratch = lambda *n: pltpu.VMEM((*n, 8, LANES), F32)
    b, h, c, last, first = call(
        pack_kernel,
        [block, block, kept(LEVELS - 1, ROWS, LANES), stack, stack],
        [right_side, helmholtz, coupling],
        [HBM] * 3,
        scratch=[pltpu.SemaphoreType.DMA((3, CHUNKS))],
        flops=10000000,
    )
    halo, lanes_e, lanes_d = call(
        edge_lanes_kernel,
        [kept(2, 4, LEVELS, 8, LANES), message, message],
        [rows_a, rows_b, last, first],
        [VMEM] * 4,
        scratch=[tile_scratch(4, STACKED), tile_scratch(2, 4, LEVELS), tile_scratch(2, 2, LEVELS)],
    )
    scaled, inverse, ratio, x0, terms, edge0, sum0, y1 = call(
        first_kernel,
        [field] * 4 + [kept(4, 8 * TILES, LANES), edges, kept(8, LANES), block],
        [b, h, c, halo],
        [VMEM] * 4,
        flops=10000000,
    )
    lanes_e = swap(lanes_e, lon_even)
    lanes_d = swap(lanes_d, lon_odd)
    y1, x1, x2, y2, y3, sums = call(
        middle_kernel,
        [block, field, field, block, block, kept(128, LANES)],
        [scaled, inverse, ratio, x0, y1, terms, lanes_e, lanes_d, edge0, sum0],
        [VMEM] * 10,
        scratch=[tile_scratch(LEVELS)] * 4 + [tile_scratch(3, LEVELS)],
        flops=100000000,
        aliases={4: 0},
    )
    sums = lax.all_to_all(sums, AXES, 0, 0, tiled=True)
    result = jax.ShapeDtypeStruct((LEVELS, ROWS, LANES), F32)
    return call(
        last_kernel,
        [result, result],
        [sums, b, x0, x1, x2, y1, y2, y3],
        [VMEM] * 8,
        out_specs=[ANY, ANY],
        scratch=[
            pltpu.VMEM((LEVELS, ROWS, LANES), F32),
            pltpu.VMEM((LEVELS, ROWS, LANES), F32),
            pltpu.SemaphoreType.DMA((2, CHUNKS)),
        ],
        flops=10000000,
    )


def solution(mesh):
    spec = P(None, "lat", "lon")
    return jax.shard_map(
        lambda *args: tuple(on_device(*args)),
        mesh=mesh,
        in_specs=(spec,) * 3,
        out_specs=(spec,) * 2,
        check_vma=False,
    )
```

```python
import functools
import math

import jax
import jax.numpy as jnp
from jax import lax
from jax.experimental import pallas as pl
from jax.experimental.pallas import tpu as pltpu
from jax.sharding import PartitionSpec as P

LEVELS = 20
ROWS = 256
LANES = 128
TOTAL_ROWS = 1024
LON_COEFF = 4.0
TILES = ROWS // 8 + 2
EXTENDED = 8 * TILES + 16
STACKED = 3 * LEVELS - 1
AT_H = LEVELS
AT_C = 2 * LEVELS
CHUNKS = 8
GROUP = 8
PARTIALS = 16
PAD = 8
LANE_MESSAGE = LEVELS + (2 * LEVELS + 1) // 3
AXES = ("lon", "lat")
F32 = jnp.float32
MIB = 1 << 20


def swap(x, partner):
    return lax.ppermute(x, AXES, [(i, partner(i)) for i in range(128)])


def lat_even(i):
    return i ^ 1


def lat_odd(i):
    lon, lat = i >> 2, i & 3
    if lat in (1, 2):
        return (lon << 2) | (3 - lat)
    return ((lon ^ 16) << 2) | lat


def lon_even(i):
    return i ^ 4


def lon_odd(i):
    lon, lat = i >> 2, i & 3
    other = (lon + 1) % 32 if lon % 2 else (lon - 1) % 32
    return (other << 2) | lat


def lane_index():
    return lax.broadcasted_iota(jnp.int32, (8, LANES), 1)


def sub_index():
    return lax.broadcasted_iota(jnp.int32, (8, LANES), 0)


def capped_cosine(row):
    angle = (row + 0.5) * (math.pi / TOTAL_ROWS) - 0.5 * math.pi
    square = angle * angle
    value = jnp.full_like(row, 0.0)
    for n in range(8, -1, -1):
        value = value * square + (-1.0) ** n / math.factorial(2 * n)
    return jnp.maximum(value, 0.5)


def row_terms(row):
    here = capped_cosine(row)
    return (
        here,
        LON_COEFF / here,
        (here + capped_cosine(row + 1.0)) * 0.5,
        (here + capped_cosine(row - 1.0)) * 0.5,
    )


def eliminate(tiles):
    count = len(tiles)
    below = [None] * count
    ratio = [None] * count
    value = [None] * count
    total = [None] * count
    for k in range(LEVELS):
        for n, (terms, right, helm, coup, store, put, get) in enumerate(tiles):
            cosine, over, north, south = terms
            pivot = cosine * helm(k) + (2.0 * over + north + south)
            scaled = cosine * coup(k) if k < LEVELS - 1 else None
            if scaled is not None:
                pivot = pivot + scaled
            if k > 0:
                pivot = (pivot + below[n]) - below[n] * ratio[n]
            inverse = 1.0 / pivot
            summed = right(k)
            if k > 0:
                summed = summed + below[n] * value[n]
            value[n] = summed * inverse
            total[n] = summed * value[n] if k == 0 else total[n] + summed * value[n]
            put(k, value[n])
            ratio[n] = scaled * inverse if scaled is not None else None
            below[n] = scaled
            store(k, scaled, inverse, ratio[n])
    for k in range(LEVELS - 2, -1, -1):
        for n, (terms, right, helm, coup, store, put, get) in enumerate(tiles):
            value[n] = get(0, k) + get(1, k) * value[n]
            put(k, value[n])
    return total


def rows_beside(x):
    above = jnp.concatenate([x[1:], pltpu.roll(x, LANES - 3, axis=1)[:1]], 0)
    below = jnp.concatenate([pltpu.roll(x, 3, axis=1)[7:], x[:7]], 0)
    return above, below


def packed_edges(read, lane):
    last = jnp.zeros((8, LANES), F32)
    first = jnp.zeros((8, LANES), F32)
    group = lane // 3
    for t in range(1, TILES - 1):
        turned = pltpu.roll(read(t), 3 * t + 3, axis=1)
        last = jnp.where(group == t, turned, last)
        first = jnp.where(group == t + 1, turned, first)
    return last, first


def edge_rows_kernel(b_lo, b_hi, h_lo, h_hi, c_lo, c_hi, o_ref, a_ref):
    lat = lax.axis_index("lat")
    even = lat % 2 == 0
    levels = [
        (at + k, lo, hi, k)
        for at, count, lo, hi in (
            (0, LEVELS, b_lo, b_hi),
            (AT_H, LEVELS, h_lo, h_hi),
            (AT_C, LEVELS - 1, c_lo, c_hi),
        )
        for k in range(count)
    ]

    def put_high(ref):
        for j, lo, hi, k in reversed(levels):
            ref[pl.ds(PAD + 3 * j - 5, 8), :] = hi[k]

    def put_low(ref):
        for j, lo, hi, k in levels:
            ref[pl.ds(PAD + 3 * j, 8), :] = lo[k]

    @pl.when(even)
    def _():
        put_high(a_ref)

    @pl.when(jnp.logical_not(even))
    def _():
        put_low(a_ref)

    @pl.when(lat == 0)
    def _():
        for j, lo, hi, k in levels:
            for i in range(3):
                o_ref[pl.ds(PAD + 3 * j + i, 1), :] = lo[k, pl.ds(2 - i, 1), :]

    @pl.when(lat == 1)
    def _():
        put_high(o_ref)

    @pl.when(lat == 2)
    def _():
        put_low(o_ref)

    @pl.when(lat == 3)
    def _():
        for j, lo, hi, k in levels:
            for i in range(3):
                o_ref[pl.ds(PAD + 3 * j + i, 1), :] = hi[k, pl.ds(7 - i, 1), :]


def pack_kernel(b_hbm, h_hbm, c_hbm, b_ref, h_ref, c_ref, last_ref, first_ref, sems):
    arrays = (
        (b_hbm, b_ref, 0, LEVELS),
        (h_hbm, h_ref, AT_H, LEVELS),
        (c_hbm, c_ref, AT_C, LEVELS - 1),
    )
    parts = []
    for i, (src, dst, at, count) in enumerate(arrays):
        for n in range(CHUNKS):
            lo, hi = count * n // CHUNKS, count * (n + 1) // CHUNKS
            levels = pl.ds(lo, hi - lo)
            copy = pltpu.make_async_copy(src.at[levels], dst.at[levels], sems.at[i, n])
            copy.start()
            parts.append((copy, dst, at, lo, hi))
    lane = lane_index()
    for copy, source, at, lo, hi in parts:
        copy.wait()

        for k in range(lo, hi):
            last, first = packed_edges(lambda t: source[k, pl.ds(8 * t - 8, 8), :], lane)
            last_ref[at + k] = last
            first_ref[at + k] = first


def first_kernel(
    b_ref, h_ref, c_ref, halo_ref, scaled_ref, inverse_ref, ratio_ref, x_ref, terms_ref, edge_ref,
    sum_ref, y_ref
):
    base = lax.axis_index("lat") * ROWS
    lane = lane_index()
    sub = sub_index()

    def row_term(t, carry):
        row = (base + 8 * t - 8 + sub).astype(F32)
        for i, term in enumerate(row_terms(row)):
            terms_ref[i, pl.ds(pl.multiple_of(8 * t, 8), 8), :] = term
        return carry

    lax.fori_loop(0, TILES, row_term, 0, unroll=2)
    for n, t in ((0, 0), (1, TILES - 1)):
        for k in range(LEVELS):
            wide = pl.ds(8 * t + 8, 8)
            x_ref[k, wide, :] = halo_ref[n, 0, k]
            inverse_ref[k, wide, :] = halo_ref[n, 2, k]
            if k < LEVELS - 1:
                scaled_ref[k, wide, :] = halo_ref[n, 1, k]
                ratio_ref[k, wide, :] = halo_ref[n, 3, k]

    group = lane // 3
    for k in range(LEVELS):
        edge_ref[k] = jnp.zeros((8, LANES), F32)

    def eliminated(g):
        work = []
        for n in range(4):
            at = pl.ds(pl.multiple_of(32 * g + 8 * n, 8), 8)
            wide = pl.ds(pl.multiple_of(32 * g + 8 * n + 16, 8), 8)
            terms = [
                terms_ref[i, pl.ds(pl.multiple_of(32 * g + 8 * n + 8, 8), 8), :] for i in range(4)
            ]

            def store(k, scaled, inverse, ratio, wide=wide):
                inverse_ref[k, wide, :] = inverse
                if scaled is not None:
                    scaled_ref[k, wide, :] = scaled
                    ratio_ref[k, wide, :] = ratio

            def put(k, value, wide=wide):
                x_ref[k, wide, :] = value

            def get(which, k, wide=wide):
                return (x_ref, ratio_ref)[which][k, wide, :]

            work.append((
                terms,
                lambda k, at=at: b_ref[k, at, :],
                lambda k, at=at: h_ref[k, at, :],
                lambda k, at=at: c_ref[k, at, :],
                store,
                put,
                get,
            ))
        return sum(eliminate(work))

    def neighbours(tiles):
        terms = [
            [terms_ref[i, pl.ds(pl.multiple_of(8 * t, 8), 8), :] for i in range(1, 4)] for t in tiles
        ]
        for k in range(LEVELS):
            edge = edge_ref[k]
            for t, (over, north, south) in zip(tiles, terms):
                start = pl.multiple_of(8 * t + 8, 8)
                wide = pl.ds(start, 8)
                x = x_ref[k, wide, :]
                west = jnp.where(lane == 0, 0.0, pltpu.roll(x, 1, axis=1))
                east = jnp.where(lane == LANES - 1, 0.0, pltpu.roll(x, LANES - 1, axis=1))
                above = x_ref[k, pl.ds(start + 1, 8), :]
                below = x_ref[k, pl.ds(start - 1, 8), :]
                y_ref[k, wide, :] = over * (west + east) + north * above + south * below
                edge = jnp.where(group == t, pltpu.roll(x, 3 * t + 2, axis=1), edge)
            edge_ref[k] = edge

    def both(g, total):
        total = total + eliminated(g)
        neighbours([4 * g - 4 + n for n in range(4)])
        return total

    sum_ref[...] = lax.fori_loop(1, ROWS // 32, both, eliminated(0))
    neighbours(range(TILES - 6, TILES))


def edge_lanes_kernel(
    o_ref, a_ref, last_ref, first_ref, halo_ref, d_ref, e_ref, raw_ref, strip_ref, part_ref
):
    even = lax.axis_index("lat") % 2 == 0
    lon_is_even = lax.axis_index("lon") % 2 == 0
    base = lax.axis_index("lat") * ROWS
    lane = lane_index()
    sub = sub_index()
    group = lane // 3
    slot = lane % 3
    for j in range(STACKED):
        low, high = pl.ds(PAD + 3 * j - 5, 8), pl.ds(PAD + 3 * j, 8)
        south = jnp.where(even, o_ref[low, :], a_ref[low, :])
        north = jnp.where(even, a_ref[high, :], o_ref[high, :])
        raw_ref[0, j] = south
        raw_ref[1, j] = north
        last, first = last_ref[j], first_ref[j]
        for t, value in ((0, south), (TILES - 1, north)):
            turned = pltpu.roll(value, 3 * t + 3, axis=1)
            last = jnp.where(group == t, turned, last)
            first = jnp.where(group == t + 1, turned, first)
        raw_ref[2, j] = last
        raw_ref[3, j] = pltpu.roll(first, LANES - 3, axis=1)
    strip_terms = row_terms((base + 8 * group - 8 + sub).astype(F32))
    work = []
    for n in range(4):
        if n < 2:
            terms = row_terms((base + (TILES - 1) * 8 * n - 8 + sub).astype(F32))
            keep = halo_ref.at[n]
        else:
            terms = strip_terms
            keep = strip_ref.at[n - 2]

        def store(k, scaled, inverse, ratio, keep=keep):
            keep[2, k] = inverse
            if scaled is not None:
                keep[1, k] = scaled
                keep[3, k] = ratio

        def put(k, value, keep=keep):
            keep[0, k] = value

        def get(which, k, keep=keep):
            return keep[3 * which, k]

        work.append((
            terms,
            lambda k, n=n: raw_ref[n, k],
            lambda k, n=n: raw_ref[n, AT_H + k],
            lambda k, n=n: raw_ref[n, AT_C + k],
            store,
            put,
            get,
        ))
    eliminate(work)
    _, over, north, south = strip_terms
    value = [None, None]
    for k in range(LEVELS):
        for side in (0, 1):
            x = strip_ref[side, 0, k]
            up = pltpu.roll(x, 1, axis=1)
            down = pltpu.roll(x, LANES - 1, axis=1)
            if side == 0:
                down = jnp.where(slot == 2, 0.0, down)
            else:
                up = jnp.where(slot == 0, 0.0, up)
            above, below = rows_beside(x)
            y = over * (up + down) + north * above + south * below
            part_ref[side, 0, k] = y
            if k > 0:
                y = y + strip_ref[side, 1, k - 1] * value[side]
            value[side] = y * strip_ref[side, 2, k]
            part_ref[side, 1, k] = value[side]
    for k in range(LEVELS - 1, -1, -1):
        messages = []
        for side in (0, 1):
            if k < LEVELS - 1:
                value[side] = part_ref[side, 1, k] + strip_ref[side, 3, k] * value[side]
            outer = 2 - 2 * side
            known = pltpu.roll(part_ref[side, 0, k], (2 - 2 * outer) % LANES, axis=1)
            message = jnp.where(slot == outer, strip_ref[side, 0, k], known)
            messages.append(jnp.where(slot == 1, value[side], message))
        last, first = messages
        e_ref[k] = jnp.where(lon_is_even, last, first)
        d_ref[k] = jnp.where(lon_is_even, first, last)
    for m in range(LEVELS, LANE_MESSAGE):
        messages = []
        for side in (0, 1):
            outer = 2 - 2 * side
            message = jnp.zeros((8, LANES), F32)
            for q in range(3):
                at = 3 * (m - LEVELS) + q
                source = strip_ref[side, 2, at] if at < LEVELS else strip_ref[side, 1, at - LEVELS]
                message = jnp.where(slot == q, pltpu.roll(source, (q - outer) % LANES, axis=1), message)
            messages.append(message)
        last, first = messages
        e_ref[m] = jnp.where(lon_is_even, last, first)
        d_ref[m] = jnp.where(lon_is_even, first, last)


def middle_kernel(
    scaled_ref, inverse_ref, ratio_ref, x0_ref, y1_in, terms_ref, d_ref, e_ref, edge0_ref, sum_ref,
    y1_ref, x1_ref, x2_ref, y2_ref, y3_ref, sums_ref, strip0_ref, strip_ref, further_ref, edge_ref,
    factor_ref
):
    del y1_in
    base = lax.axis_index("lat") * ROWS
    lon_is_even = lax.axis_index("lon") % 2 == 0
    lane = lane_index()
    sub = sub_index()
    slot = lane % 3
    group = lane // 3
    _, strip_over, strip_north, strip_south = row_terms((base + 8 * group - 8 + sub).astype(F32))

    def turned(x, by):
        return pltpu.roll(x, by % LANES, axis=1) if by % LANES else x

    def arrived(m):
        e, d = e_ref[m], d_ref[m]
        return jnp.where(lon_is_even, d, e), jnp.where(lon_is_even, e, d)

    for m in range(LEVELS, LANE_MESSAGE):
        left, right = arrived(m)
        for q in range(3):
            at = 3 * (m - LEVELS) + q
            value = jnp.where(slot == 2, turned(left, 2 - q), turned(right, 1 - q))
            if at < LEVELS:
                factor_ref[1, at] = value
            else:
                factor_ref[0, at - LEVELS] = value
    for k in range(LEVELS - 1):
        factor_ref[2, k] = factor_ref[0, k] * factor_ref[1, k]

    def solve_strip(right, out_ref):
        value = None
        for k in range(LEVELS):
            y = right(k)
            if k > 0:
                y = y + factor_ref[0, k - 1] * value
            value = y * factor_ref[1, k]
            out_ref[k] = value
        for k in range(LEVELS - 2, -1, -1):
            value = out_ref[k] + factor_ref[2, k] * value
            out_ref[k] = value

    def first_right(k):
        left, right = arrived(k)
        strip0_ref[k] = jnp.where(slot == 2, left, turned(right, 1))
        further_ref[k] = jnp.where(slot == 2, turned(left, 1), right)
        known = jnp.where(slot == 2, turned(left, 2), turned(right, -1))
        return known + strip_over * edge0_ref[k]

    def second_right(k):
        above, below = rows_beside(strip_ref[k])
        beside = further_ref[k] + edge_ref[k]
        return strip_over * beside + strip_north * above + strip_south * below

    def step(tiles, x_ref, y_ref, out_ref, halo_ref, sums, begun=False):
        starts = [pl.multiple_of(8 * t + 8, 8) for t in tiles]
        wides = [pl.ds(start, 8) for start in starts]
        ats = wides if begun else [pl.ds(pl.multiple_of(8 * t - 8, 8), 8) for t in tiles]
        terms = [
            [terms_ref[i, pl.ds(pl.multiple_of(8 * t, 8), 8), :] for i in range(1, 4)] for t in tiles
        ]
        zero = jnp.zeros((8, LANES), F32)
        cross = [zero] * len(tiles)
        own = [zero] * len(tiles)
        forward = [[] for _ in tiles]
        for k in range(LEVELS):
            for n, t in enumerate(tiles):
                over, north, south = terms[n]
                x = x_ref[k, wides[n], :]
                inject = pltpu.roll(halo_ref[k], 126 - 3 * t, axis=1)
                if begun:
                    inject = jnp.where((lane == 0) | (lane == LANES - 1), inject, 0.0)
                    y = y_ref[k, ats[n], :] + over * inject
                else:
                    west = jnp.where(lane == 0, inject, pltpu.roll(x, 1, axis=1))
                    east = jnp.where(lane == LANES - 1, inject, pltpu.roll(x, LANES - 1, axis=1))
                    above = x_ref[k, pl.ds(starts[n] + 1, 8), :]
                    below = x_ref[k, pl.ds(starts[n] - 1, 8), :]
                    y = over * (west + east) + north * above + south * below
                if sums is not None:
                    y_ref[k, ats[n], :] = y
                    cross[n] = cross[n] + x * y
                if k > 0:
                    y = y + scaled_ref[k - 1, wides[n], :] * forward[n][-1]
                value = y * inverse_ref[k, wides[n], :]
                if sums is not None:
                    own[n] = own[n] + y * value
                forward[n].append(value)
        if out_ref is not None:
            value = [f[-1] for f in forward]
            for k in range(LEVELS - 1, -1, -1):
                edge = edge_ref[k] if begun else None
                for n, t in enumerate(tiles):
                    if k < LEVELS - 1:
                        value[n] = forward[n][k] + ratio_ref[k, wides[n], :] * value[n]
                    out_ref[k, wides[n], :] = value[n]
                    if begun:
                        edge = jnp.where(group == t, pltpu.roll(value[n], 3 * t + 2, axis=1), edge)
                if begun:
                    edge_ref[k] = edge
        if sums is not None:
            return sums[0] + sum(cross), sums[1] + sum(own)

    zero = jnp.zeros((8, LANES), F32)
    totals = [sum_ref[...]]
    for k in range(LEVELS):
        edge_ref[k] = zero
    solve_strip(first_right, strip_ref)
    for x_ref, y_ref, out_ref, halo_ref in (
        (x0_ref, y1_ref, x1_ref, strip0_ref),
        (x1_ref, y2_ref, x2_ref, strip_ref),
        (x2_ref, y3_ref, None, strip_ref),
    ):
        totals += lax.fori_loop(
            0,
            ROWS // 8 // GROUP,
            lambda g, sums: step(
                [GROUP * g + n + 1 for n in range(GROUP)], x_ref, y_ref, out_ref, halo_ref, sums,
                x_ref is x0_ref
            ),
            (zero, zero),
        )
        if out_ref is not None:
            begun = x_ref is x0_ref
            step([0, TILES - 1], x_ref, y_ref, out_ref, halo_ref, None, begun)
        if x_ref is x1_ref:
            solve_strip(second_right, strip_ref)
    row = zero[:1]
    for n, total in enumerate(totals):
        part = jnp.sum(total, axis=0, keepdims=True)
        for by in (64, 32, 16):
            part = part + pltpu.roll(part, by, axis=1)
        row = jnp.where(lane[:1] // PARTIALS == n, part, row)
    sums_ref[...] = jnp.broadcast_to(row, sums_ref.shape)


def two_sum(a, b):
    total = a + b
    part = total - a
    return total, (a - (total - part)) + (b - part)


def coefficients(parts):
    pairs = [(part, None) for part in parts]
    while len(pairs) > 1:
        joined = []
        for (a, a_low), (b, b_low) in zip(pairs[::2], pairs[1::2]):
            total, error = two_sum(a, b)
            joined.append((total, error if a_low is None else (a_low + b_low) + error))
        pairs = joined
    high, low = pairs[0]
    for axis, by in ((0, 4), (0, 2), (0, 1), (1, 8), (1, 4), (1, 2), (1, 1)):
        by = high.shape[axis] - by
        high, error = two_sum(high, pltpu.roll(high, by, axis=axis))
        low = (low + pltpu.roll(low, by, axis=axis)) + error
    spread = lambda x: jnp.concatenate(
        [jnp.broadcast_to(x[:1, PARTIALS * n : PARTIALS * n + 1], (1, LANES)) for n in range(8)], 0
    )
    high, low = spread(high), spread(low)
    row = lambda x, n: jnp.broadcast_to(x[n : n + 1], (8, LANES))
    shift = jnp.floor(64.0 * (row(high, 1) / row(high, 0)) + 0.5) * (1.0 / 64.0)
    centred = []
    for n in range(7):
        centred.append(row(high, 0) + row(low, 0))
        if n == 6:
            break
        wide = 4097.0 * high
        coarse = wide - (wide - high)
        fine = high - coarse
        following = jnp.concatenate([high[1:], high[:1]], 0)
        rest = jnp.concatenate([low[1:], low[:1]], 0) - shift * low
        total, error = two_sum(following, -shift * coarse)
        rest = rest + error
        total, error = two_sum(total, -shift * fine)
        rest = rest + error
        high = total + rest
        low = rest - (high - total)
    sigma = 1.0 - shift
    energies = [sigma * centred[n] - centred[n + 1] for n in range(6)]
    curvatures = [sigma * energies[n] - energies[n + 1] for n in range(5)]

    def product(p, q, table):
        return sum(p[i] * q[j] * table[i + j] for i in range(len(p)) for j in range(len(q)))

    one = jnp.ones((8, LANES), F32)
    none = jnp.zeros((8, LANES), F32)
    smoothed = [one]
    direction = [one]
    result = []
    energy = energies[0]
    for iteration in range(3):
        length = energy / product(direction, direction, curvatures)
        result = [
            (result[i] if i < len(result) else none) + length * direction[i]
            for i in range(len(direction))
        ]
        if iteration < 2:
            image = [sigma * d for d in direction] + [none]
            image = [image[i] - (direction[i - 1] if i else none) for i in range(len(image))]
            smoothed = [
                (smoothed[i] if i < len(smoothed) else none) - length * image[i]
                for i in range(len(image))
            ]
            following = product(smoothed, smoothed, energies)
            ratio = following / energy
            direction = [
                smoothed[i] + (ratio * direction[i] if i < len(direction) else none)
                for i in range(len(smoothed))
            ]
            energy = following
    k0, k1, k2 = result
    return k0 - shift * k1 + shift * shift * k2, k1 - 2.0 * shift * k2, k2


def last_kernel(
    sums_ref, b_ref, x0_ref, x1_ref, x2_ref, y1_ref, y2_ref, y3_ref, solution_hbm, residual_hbm,
    solution_ref, residual_ref, sems
):
    step = ROWS // CHUNKS
    k0, k1, k2 = coefficients([sums_ref[8 * n : 8 * n + 8] for n in range(16)])
    r0, r1, r2 = 1.0 - k0, k0 - k1, k1 - k2

    def copy(i, n):
        src = (solution_ref, residual_ref)[i]
        dst = (solution_hbm, residual_hbm)[i]
        rows = pl.ds(n * step, step)
        return pltpu.make_async_copy(src.at[:, rows, :], dst.at[:, rows, :], sems.at[i, n])

    for n in range(CHUNKS):

        def tile(t, carry):
            at = pl.ds(pl.multiple_of(8 * t - 8, 8), 8)
            wide = pl.ds(pl.multiple_of(8 * t + 8, 8), 8)
            for k in range(LEVELS):
                solution_ref[k, at, :] = (
                    k0 * x0_ref[k, wide, :] + k1 * x1_ref[k, wide, :] + k2 * x2_ref[k, wide, :]
                )
                residual_ref[k, at, :] = (
                    r0 * b_ref[k, at, :] + r1 * y1_ref[k, wide, :]
                    + r2 * y2_ref[k, at, :] + k2 * y3_ref[k, at, :]
                )
            return carry

        lax.fori_loop(1 + n * step // 8, 1 + (n + 1) * step // 8, tile, 0)
        for i in range(2):
            copy(i, n).start()
    for n in range(CHUNKS):
        for i in range(2):
            copy(i, n).wait()


VMEM = pl.BlockSpec(memory_space=pltpu.VMEM)
ANY = pl.BlockSpec(memory_space=pl.ANY)
HBM = pl.BlockSpec(memory_space=pltpu.HBM)


def kept(*shape):
    return pltpu.VMEM(shape, F32)


def call(kernel, outs, ins, in_specs, out_specs=None, scratch=(), limit=8, flops=0, aliases=None):
    return pl.pallas_call(
        kernel,
        out_shape=outs,
        in_specs=in_specs,
        out_specs=[VMEM] * len(outs) if out_specs is None else out_specs,
        scratch_shapes=list(scratch),
        input_output_aliases=aliases or {},
        compiler_params=pltpu.CompilerParams(vmem_limit_bytes=limit * MIB),
        cost_estimate=pl.CostEstimate(flops=flops, bytes_accessed=1000000, transcendentals=0),
        name=kernel.__name__,
    )(*ins)


def on_device(right_side, helmholtz, coupling):
    right_side, helmholtz, coupling = [
        pltpu.with_memory_space_constraint(x, pltpu.HBM) for x in (right_side, helmholtz, coupling)
    ]
    low = pl.BlockSpec((LEVELS, 8, LANES), lambda i: (0, 0, 0))
    high = pl.BlockSpec((LEVELS, 8, LANES), lambda i: (0, ROWS // 8 - 1, 0))
    low_c = pl.BlockSpec((LEVELS - 1, 8, LANES), lambda i: (0, 0, 0))
    high_c = pl.BlockSpec((LEVELS - 1, 8, LANES), lambda i: (0, ROWS // 8 - 1, 0))
    message_rows = -(-(PAD + 3 * STACKED + 5) // 8) * 8
    rows_b, rows_a = pl.pallas_call(
        edge_rows_kernel,
        grid=(1,),
        out_shape=[kept(message_rows, LANES)] * 2,
        in_specs=[low, high, low, high, low_c, high_c],
        out_specs=[pl.BlockSpec((message_rows, LANES), lambda i: (0, 0))] * 2,
        name="edge_rows",
    )(right_side, right_side, helmholtz, helmholtz, coupling, coupling)
    rows_b = swap(rows_b, lat_odd)
    rows_a = swap(rows_a, lat_even)
    field = kept(LEVELS, EXTENDED, LANES)
    block = kept(LEVELS, ROWS, LANES)
    stack = kept(STACKED, 8, LANES)
    edges = kept(LEVELS, 8, LANES)
    message = kept(LANE_MESSAGE, 8, LANES)
    tile_scratch = lambda *n: pltpu.VMEM((*n, 8, LANES), F32)
    b, h, c, last, first = call(
        pack_kernel,
        [block, block, kept(LEVELS - 1, ROWS, LANES), stack, stack],
        [right_side, helmholtz, coupling],
        [HBM] * 3,
        scratch=[pltpu.SemaphoreType.DMA((3, CHUNKS))],
        flops=10000000,
    )
    halo, lanes_d, lanes_e = call(
        edge_lanes_kernel,
        [kept(2, 4, LEVELS, 8, LANES), message, message],
        [rows_b, rows_a, last, first],
        [VMEM] * 4,
        scratch=[tile_scratch(4, STACKED), tile_scratch(2, 4, LEVELS), tile_scratch(2, 2, LEVELS)],
    )
    scaled, inverse, ratio, x0, terms, edge0, sum0, y1 = call(
        first_kernel,
        [field] * 4 + [kept(4, 8 * TILES, LANES), edges, kept(8, LANES), field],
        [b, h, c, halo],
        [VMEM] * 4,
        flops=10000000,
    )
    lanes_d = swap(lanes_d, lon_odd)
    lanes_e = swap(lanes_e, lon_even)
    y1, x1, x2, y2, y3, sums = call(
        middle_kernel,
        [field, field, field, block, block, kept(128, LANES)],
        [scaled, inverse, ratio, x0, y1, terms, lanes_d, lanes_e, edge0, sum0],
        [VMEM] * 10,
        scratch=[tile_scratch(LEVELS)] * 4 + [tile_scratch(3, LEVELS)],
        flops=100000000,
        aliases={4: 0},
    )
    sums = lax.all_to_all(sums, AXES, 0, 0, tiled=True)
    result = jax.ShapeDtypeStruct((LEVELS, ROWS, LANES), F32)
    return call(
        last_kernel,
        [result, result],
        [sums, b, x0, x1, x2, y1, y2, y3],
        [VMEM] * 8,
        out_specs=[ANY, ANY],
        scratch=[
            pltpu.VMEM((LEVELS, ROWS, LANES), F32),
            pltpu.VMEM((LEVELS, ROWS, LANES), F32),
            pltpu.SemaphoreType.DMA((2, CHUNKS)),
        ],
        flops=10000000,
    )


def solution(mesh):
    spec = P(None, "lat", "lon")
    return jax.shard_map(
        lambda *args: tuple(on_device(*args)),
        mesh=mesh,
        in_specs=(spec,) * 3,
        out_specs=(spec,) * 2,
        check_vma=False,
    )
```

```python
import functools
import math

import jax
import jax.numpy as jnp
from jax import lax
from jax.experimental import pallas as pl
from jax.experimental.pallas import tpu as pltpu
from jax.sharding import PartitionSpec as P

LEVELS = 20
ROWS = 256
LANES = 128
TOTAL_ROWS = 1024
LON_COEFF = 4.0
TILES = ROWS // 8 + 2
EXTENDED = 8 * TILES + 16
STACKED = 3 * LEVELS - 1
AT_H = LEVELS
AT_C = 2 * LEVELS
CHUNKS = 8
PACKS = 2
GROUP = 16
PARTIALS = 16
PAD = 8
LANE_MESSAGE = LEVELS + (2 * LEVELS + 1) // 3
AXES = ("lon", "lat")
F32 = jnp.float32
MIB = 1 << 20


def swap(x, partner):
    return lax.ppermute(x, AXES, [(i, partner(i)) for i in range(128)])


def lat_even(i):
    return i ^ 1


def lat_odd(i):
    lon, lat = i >> 2, i & 3
    if lat in (1, 2):
        return (lon << 2) | (3 - lat)
    return ((lon ^ 16) << 2) | lat


def lon_even(i):
    return i ^ 4


def lon_odd(i):
    lon, lat = i >> 2, i & 3
    other = (lon + 1) % 32 if lon % 2 else (lon - 1) % 32
    return (other << 2) | lat


def lane_index():
    return lax.broadcasted_iota(jnp.int32, (8, LANES), 1)


def sub_index():
    return lax.broadcasted_iota(jnp.int32, (8, LANES), 0)


def capped_cosine(row):
    angle = (row + 0.5) * (math.pi / TOTAL_ROWS) - 0.5 * math.pi
    square = angle * angle
    value = jnp.full_like(row, 0.0)
    for n in range(8, -1, -1):
        value = value * square + (-1.0) ** n / math.factorial(2 * n)
    return jnp.maximum(value, 0.5)


def row_terms(row):
    here = capped_cosine(row)
    return (
        here,
        LON_COEFF / here,
        (here + capped_cosine(row + 1.0)) * 0.5,
        (here + capped_cosine(row - 1.0)) * 0.5,
    )


def eliminate(tiles):
    count = len(tiles)
    below = [None] * count
    ratio = [None] * count
    value = [None] * count
    total = [None] * count
    for k in range(LEVELS):
        for n, (terms, right, helm, coup, store, put, get) in enumerate(tiles):
            cosine, over, north, south = terms
            pivot = cosine * helm(k) + (2.0 * over + north + south)
            scaled = cosine * coup(k) if k < LEVELS - 1 else None
            if scaled is not None:
                pivot = pivot + scaled
            if k > 0:
                pivot = (pivot + below[n]) - below[n] * ratio[n]
            inverse = 1.0 / pivot
            summed = right(k)
            if k > 0:
                summed = summed + below[n] * value[n]
            value[n] = summed * inverse
            total[n] = summed * value[n] if k == 0 else total[n] + summed * value[n]
            put(k, value[n])
            ratio[n] = scaled * inverse if scaled is not None else None
            below[n] = scaled
            store(k, scaled, inverse, ratio[n])
    for k in range(LEVELS - 2, -1, -1):
        for n, (terms, right, helm, coup, store, put, get) in enumerate(tiles):
            value[n] = get(0, k) + get(1, k) * value[n]
            put(k, value[n])
    return total


def rows_beside(x):
    above = jnp.concatenate([x[1:], pltpu.roll(x, LANES - 3, axis=1)[:1]], 0)
    below = jnp.concatenate([pltpu.roll(x, 3, axis=1)[7:], x[:7]], 0)
    return above, below


def packed_edges(read, lane):
    last = jnp.zeros((8, LANES), F32)
    first = jnp.zeros((8, LANES), F32)
    group = lane // 3
    for t in range(1, TILES - 1):
        turned = pltpu.roll(read(t), 3 * t + 3, axis=1)
        last = jnp.where(group == t, turned, last)
        first = jnp.where(group == t + 1, turned, first)
    return last, first


def edge_rows_kernel(b_lo, b_hi, h_lo, h_hi, c_lo, c_hi, o_ref, a_ref):
    lat = lax.axis_index("lat")
    even = lat % 2 == 0
    levels = [
        (at + k, lo, hi, k)
        for at, count, lo, hi in (
            (0, LEVELS, b_lo, b_hi),
            (AT_H, LEVELS, h_lo, h_hi),
            (AT_C, LEVELS - 1, c_lo, c_hi),
        )
        for k in range(count)
    ]

    def put_high(ref):
        for j, lo, hi, k in reversed(levels):
            ref[pl.ds(PAD + 3 * j - 5, 8), :] = hi[k]

    def put_low(ref):
        for j, lo, hi, k in levels:
            ref[pl.ds(PAD + 3 * j, 8), :] = lo[k]

    @pl.when(even)
    def _():
        put_high(a_ref)

    @pl.when(jnp.logical_not(even))
    def _():
        put_low(a_ref)

    @pl.when(lat == 0)
    def _():
        for j, lo, hi, k in levels:
            for i in range(3):
                o_ref[pl.ds(PAD + 3 * j + i, 1), :] = lo[k, pl.ds(2 - i, 1), :]

    @pl.when(lat == 1)
    def _():
        put_high(o_ref)

    @pl.when(lat == 2)
    def _():
        put_low(o_ref)

    @pl.when(lat == 3)
    def _():
        for j, lo, hi, k in levels:
            for i in range(3):
                o_ref[pl.ds(PAD + 3 * j + i, 1), :] = hi[k, pl.ds(7 - i, 1), :]


def pack_kernel(b_hbm, h_hbm, c_hbm, b_ref, h_ref, c_ref, last_ref, first_ref, terms_ref, sems):
    arrays = (
        (b_hbm, b_ref, 0, LEVELS),
        (h_hbm, h_ref, AT_H, LEVELS),
        (c_hbm, c_ref, AT_C, LEVELS - 1),
    )
    parts = []
    for i, (src, dst, at, count) in enumerate(arrays):
        for n in range(PACKS):
            lo, hi = count * n // PACKS, count * (n + 1) // PACKS
            levels = pl.ds(lo, hi - lo)
            copy = pltpu.make_async_copy(src.at[levels], dst.at[levels], sems.at[i, n])
            copy.start()
            parts.append((copy, dst, at, lo, hi))
    lane = lane_index()
    sub = sub_index()
    base = lax.axis_index("lat") * ROWS
    for n, (copy, source, at, lo, hi) in enumerate(parts):
        copy.wait()
        for t in range(n, TILES, len(parts)):
            for i, term in enumerate(row_terms((base + 8 * t - 8 + sub).astype(F32))):
                terms_ref[i, pl.ds(8 * t, 8), :] = term
        for k in range(lo, hi):
            last, first = packed_edges(lambda t: source[k, pl.ds(8 * t - 8, 8), :], lane)
            last_ref[at + k] = last
            first_ref[at + k] = first


def first_kernel(
    b_ref, h_ref, c_ref, halo_ref, terms_ref, scaled_ref, inverse_ref, ratio_ref, x_ref, edge_ref,
    sum_ref, y_ref
):
    lane = lane_index()
    for n, t in ((0, 0), (1, TILES - 1)):
        for k in range(LEVELS):
            wide = pl.ds(8 * t + 8, 8)
            x_ref[k, wide, :] = halo_ref[n, 0, k]
            inverse_ref[k, wide, :] = halo_ref[n, 2, k]
            if k < LEVELS - 1:
                scaled_ref[k, wide, :] = halo_ref[n, 1, k]
                ratio_ref[k, wide, :] = halo_ref[n, 3, k]

    group = lane // 3
    for k in range(LEVELS):
        edge_ref[k] = jnp.zeros((8, LANES), F32)

    def eliminated(g):
        work = []
        for n in range(4):
            at = pl.ds(pl.multiple_of(32 * g + 8 * n, 8), 8)
            wide = pl.ds(pl.multiple_of(32 * g + 8 * n + 16, 8), 8)
            terms = [
                terms_ref[i, pl.ds(pl.multiple_of(32 * g + 8 * n + 8, 8), 8), :] for i in range(4)
            ]

            def store(k, scaled, inverse, ratio, wide=wide):
                inverse_ref[k, wide, :] = inverse
                if scaled is not None:
                    scaled_ref[k, wide, :] = scaled
                    ratio_ref[k, wide, :] = ratio

            def put(k, value, wide=wide):
                x_ref[k, wide, :] = value

            def get(which, k, wide=wide):
                return (x_ref, ratio_ref)[which][k, wide, :]

            work.append((
                terms,
                lambda k, at=at: b_ref[k, at, :],
                lambda k, at=at: h_ref[k, at, :],
                lambda k, at=at: c_ref[k, at, :],
                store,
                put,
                get,
            ))
        return sum(eliminate(work))

    def neighbours(tiles):
        terms = [
            [terms_ref[i, pl.ds(pl.multiple_of(8 * t, 8), 8), :] for i in range(1, 4)] for t in tiles
        ]
        for k in range(LEVELS):
            edge = edge_ref[k]
            for t, (over, north, south) in zip(tiles, terms):
                start = pl.multiple_of(8 * t + 8, 8)
                wide = pl.ds(start, 8)
                x = x_ref[k, wide, :]
                west = jnp.where(lane == 0, 0.0, pltpu.roll(x, 1, axis=1))
                east = jnp.where(lane == LANES - 1, 0.0, pltpu.roll(x, LANES - 1, axis=1))
                above = x_ref[k, pl.ds(start + 1, 8), :]
                below = x_ref[k, pl.ds(start - 1, 8), :]
                y_ref[k, wide, :] = over * (west + east) + north * above + south * below
                edge = jnp.where(group == t, pltpu.roll(x, 3 * t + 2, axis=1), edge)
            edge_ref[k] = edge

    def both(g, total):
        total = total + eliminated(g)
        neighbours([4 * g - 4 + n for n in range(4)])
        return total

    sum_ref[...] = lax.fori_loop(1, ROWS // 32, both, eliminated(0))
    neighbours(range(TILES - 6, TILES))


def edge_lanes_kernel(
    o_ref, a_ref, last_ref, first_ref, halo_ref, d_ref, e_ref, raw_ref, strip_ref, part_ref
):
    even = lax.axis_index("lat") % 2 == 0
    lon_is_even = lax.axis_index("lon") % 2 == 0
    base = lax.axis_index("lat") * ROWS
    lane = lane_index()
    sub = sub_index()
    group = lane // 3
    slot = lane % 3
    for j in range(STACKED):
        low, high = pl.ds(PAD + 3 * j - 5, 8), pl.ds(PAD + 3 * j, 8)
        south = jnp.where(even, o_ref[low, :], a_ref[low, :])
        north = jnp.where(even, a_ref[high, :], o_ref[high, :])
        raw_ref[0, j] = south
        raw_ref[1, j] = north
        last, first = last_ref[j], first_ref[j]
        for t, value in ((0, south), (TILES - 1, north)):
            turned = pltpu.roll(value, 3 * t + 3, axis=1)
            last = jnp.where(group == t, turned, last)
            first = jnp.where(group == t + 1, turned, first)
        raw_ref[2, j] = last
        raw_ref[3, j] = pltpu.roll(first, LANES - 3, axis=1)
    strip_terms = row_terms((base + 8 * group - 8 + sub).astype(F32))
    work = []
    for n in range(4):
        if n < 2:
            terms = row_terms((base + (TILES - 1) * 8 * n - 8 + sub).astype(F32))
            keep = halo_ref.at[n]
        else:
            terms = strip_terms
            keep = strip_ref.at[n - 2]

        def store(k, scaled, inverse, ratio, keep=keep):
            keep[2, k] = inverse
            if scaled is not None:
                keep[1, k] = scaled
                keep[3, k] = ratio

        def put(k, value, keep=keep):
            keep[0, k] = value

        def get(which, k, keep=keep):
            return keep[3 * which, k]

        work.append((
            terms,
            lambda k, n=n: raw_ref[n, k],
            lambda k, n=n: raw_ref[n, AT_H + k],
            lambda k, n=n: raw_ref[n, AT_C + k],
            store,
            put,
            get,
        ))
    eliminate(work)
    _, over, north, south = strip_terms
    value = [None, None]
    for k in range(LEVELS):
        for side in (0, 1):
            x = strip_ref[side, 0, k]
            up = pltpu.roll(x, 1, axis=1)
            down = pltpu.roll(x, LANES - 1, axis=1)
            if side == 0:
                down = jnp.where(slot == 2, 0.0, down)
            else:
                up = jnp.where(slot == 0, 0.0, up)
            above, below = rows_beside(x)
            y = over * (up + down) + north * above + south * below
            part_ref[side, 0, k] = y
            if k > 0:
                y = y + strip_ref[side, 1, k - 1] * value[side]
            value[side] = y * strip_ref[side, 2, k]
            part_ref[side, 1, k] = value[side]
    for k in range(LEVELS - 1, -1, -1):
        messages = []
        for side in (0, 1):
            if k < LEVELS - 1:
                value[side] = part_ref[side, 1, k] + strip_ref[side, 3, k] * value[side]
            outer = 2 - 2 * side
            known = pltpu.roll(part_ref[side, 0, k], (2 - 2 * outer) % LANES, axis=1)
            message = jnp.where(slot == outer, strip_ref[side, 0, k], known)
            messages.append(jnp.where(slot == 1, value[side], message))
        last, first = messages
        e_ref[k] = jnp.where(lon_is_even, last, first)
        d_ref[k] = jnp.where(lon_is_even, first, last)
    for m in range(LEVELS, LANE_MESSAGE):
        messages = []
        for side in (0, 1):
            outer = 2 - 2 * side
            message = jnp.zeros((8, LANES), F32)
            for q in range(3):
                at = 3 * (m - LEVELS) + q
                source = strip_ref[side, 2, at] if at < LEVELS else strip_ref[side, 1, at - LEVELS]
                message = jnp.where(slot == q, pltpu.roll(source, (q - outer) % LANES, axis=1), message)
            messages.append(message)
        last, first = messages
        e_ref[m] = jnp.where(lon_is_even, last, first)
        d_ref[m] = jnp.where(lon_is_even, first, last)


def middle_kernel(
    scaled_ref, inverse_ref, ratio_ref, x0_ref, y1_in, terms_ref, d_ref, e_ref, edge0_ref, sum_ref,
    y1_ref, x1_ref, x2_ref, y2_ref, y3_ref, sums_ref, strip0_ref, strip_ref, strip2_ref, further_ref,
    edge_ref, factor_ref
):
    del y1_in
    base = lax.axis_index("lat") * ROWS
    lon_is_even = lax.axis_index("lon") % 2 == 0
    lane = lane_index()
    sub = sub_index()
    slot = lane % 3
    group = lane // 3
    _, strip_over, strip_north, strip_south = row_terms((base + 8 * group - 8 + sub).astype(F32))

    def turned(x, by):
        return pltpu.roll(x, by % LANES, axis=1) if by % LANES else x

    def arrived(m):
        e, d = e_ref[m], d_ref[m]
        return jnp.where(lon_is_even, d, e), jnp.where(lon_is_even, e, d)

    for m in range(LEVELS, LANE_MESSAGE):
        left, right = arrived(m)
        for q in range(3):
            at = 3 * (m - LEVELS) + q
            value = jnp.where(slot == 2, turned(left, 2 - q), turned(right, 1 - q))
            if at < LEVELS:
                factor_ref[1, at] = value
            else:
                factor_ref[0, at - LEVELS] = value
    for k in range(LEVELS - 1):
        factor_ref[2, k] = factor_ref[0, k] * factor_ref[1, k]

    def solve_strip(right, out_ref):
        value = None
        for k in range(LEVELS):
            y = right(k)
            if k > 0:
                y = y + factor_ref[0, k - 1] * value
            value = y * factor_ref[1, k]
            out_ref[k] = value
        for k in range(LEVELS - 2, -1, -1):
            value = out_ref[k] + factor_ref[2, k] * value
            out_ref[k] = value

    def first_right(k):
        left, right = arrived(k)
        strip0_ref[k] = jnp.where(slot == 2, left, turned(right, 1))
        further_ref[k] = jnp.where(slot == 2, turned(left, 1), right)
        known = jnp.where(slot == 2, turned(left, 2), turned(right, -1))
        return known + strip_over * edge0_ref[k]

    def second_right(k):
        above, below = rows_beside(strip_ref[k])
        beside = further_ref[k] + edge_ref[k]
        return strip_over * beside + strip_north * above + strip_south * below

    def step(tiles, x_ref, y_ref, out_ref, halo_ref, sums, begun=False):
        starts = [pl.multiple_of(8 * t + 8, 8) for t in tiles]
        wides = [pl.ds(start, 8) for start in starts]
        ats = wides if begun else [pl.ds(pl.multiple_of(8 * t - 8, 8), 8) for t in tiles]
        terms = [
            [terms_ref[i, pl.ds(pl.multiple_of(8 * t, 8), 8), :] for i in range(1, 4)] for t in tiles
        ]
        zero = jnp.zeros((8, LANES), F32)
        cross = [zero] * len(tiles)
        own = [zero] * len(tiles)
        forward = [[] for _ in tiles]
        for k in range(LEVELS):
            for n, t in enumerate(tiles):
                over, north, south = terms[n]
                x = x_ref[k, wides[n], :]
                inject = pltpu.roll(halo_ref[k], 126 - 3 * t, axis=1)
                if begun:
                    inject = jnp.where((lane == 0) | (lane == LANES - 1), inject, 0.0)
                    y = y_ref[k, ats[n], :] + over * inject
                else:
                    west = jnp.where(lane == 0, inject, pltpu.roll(x, 1, axis=1))
                    east = jnp.where(lane == LANES - 1, inject, pltpu.roll(x, LANES - 1, axis=1))
                    above = x_ref[k, pl.ds(starts[n] + 1, 8), :]
                    below = x_ref[k, pl.ds(starts[n] - 1, 8), :]
                    y = over * (west + east) + north * above + south * below
                if sums is not None:
                    y_ref[k, ats[n], :] = y
                    cross[n] = cross[n] + x * y
                if k > 0:
                    y = y + scaled_ref[k - 1, wides[n], :] * forward[n][-1]
                value = y * inverse_ref[k, wides[n], :]
                if sums is not None:
                    own[n] = own[n] + y * value
                forward[n].append(value)
        if out_ref is not None:
            value = [f[-1] for f in forward]
            for k in range(LEVELS - 1, -1, -1):
                edge = edge_ref[k] if begun else None
                for n, t in enumerate(tiles):
                    if k < LEVELS - 1:
                        value[n] = forward[n][k] + ratio_ref[k, wides[n], :] * value[n]
                    out_ref[k, wides[n], :] = value[n]
                    if begun:
                        edge = jnp.where(group == t, pltpu.roll(value[n], 3 * t + 2, axis=1), edge)
                if begun:
                    edge_ref[k] = edge
        if sums is not None:
            return sums[0] + sum(cross), sums[1] + sum(own)

    zero = jnp.zeros((8, LANES), F32)
    totals = [sum_ref[...]]
    for k in range(LEVELS):
        edge_ref[k] = zero
    solve_strip(first_right, strip_ref)
    for x_ref, y_ref, out_ref, halo_ref in (
        (x0_ref, y1_ref, x1_ref, strip0_ref),
        (x1_ref, y2_ref, x2_ref, strip_ref),
        (x2_ref, y3_ref, None, strip2_ref),
    ):
        begun = x_ref is x0_ref
        if out_ref is not None:
            step([0, TILES - 1], x_ref, y_ref, out_ref, halo_ref, None, begun)
        if x_ref is x1_ref:
            solve_strip(second_right, strip2_ref)
        totals += lax.fori_loop(
            0,
            ROWS // 8 // GROUP,
            lambda g, sums: step(
                [GROUP * g + n + 1 for n in range(GROUP)], x_ref, y_ref, out_ref, halo_ref, sums, begun
            ),
            (zero, zero),
        )
    row = zero[:1]
    for n, total in enumerate(totals):
        part = jnp.sum(total, axis=0, keepdims=True)
        for by in (64, 32, 16):
            part = part + pltpu.roll(part, by, axis=1)
        row = jnp.where(lane[:1] // PARTIALS == n, part, row)
    sums_ref[...] = jnp.broadcast_to(row, sums_ref.shape)


def two_sum(a, b):
    total = a + b
    part = total - a
    return total, (a - (total - part)) + (b - part)


def coefficients(parts):
    pairs = [(part, None) for part in parts]
    while len(pairs) > 1:
        joined = []
        for (a, a_low), (b, b_low) in zip(pairs[::2], pairs[1::2]):
            total, error = two_sum(a, b)
            joined.append((total, error if a_low is None else (a_low + b_low) + error))
        pairs = joined
    high, low = pairs[0]
    for axis, by in ((0, 4), (0, 2), (0, 1), (1, 8), (1, 4), (1, 2), (1, 1)):
        by = high.shape[axis] - by
        high, error = two_sum(high, pltpu.roll(high, by, axis=axis))
        low = (low + pltpu.roll(low, by, axis=axis)) + error
    spread = lambda x: jnp.concatenate(
        [jnp.broadcast_to(x[:1, PARTIALS * n : PARTIALS * n + 1], (1, LANES)) for n in range(8)], 0
    )
    high, low = spread(high), spread(low)
    row = lambda x, n: jnp.broadcast_to(x[n : n + 1], (8, LANES))
    shift = jnp.floor(64.0 * (row(high, 1) / row(high, 0)) + 0.5) * (1.0 / 64.0)
    centred = []
    for n in range(7):
        centred.append(row(high, 0) + row(low, 0))
        if n == 6:
            break
        wide = 4097.0 * high
        coarse = wide - (wide - high)
        fine = high - coarse
        following = jnp.concatenate([high[1:], high[:1]], 0)
        rest = jnp.concatenate([low[1:], low[:1]], 0) - shift * low
        total, error = two_sum(following, -shift * coarse)
        rest = rest + error
        total, error = two_sum(total, -shift * fine)
        rest = rest + error
        high = total + rest
        low = rest - (high - total)
    sigma = 1.0 - shift
    energies = [sigma * centred[n] - centred[n + 1] for n in range(6)]
    curvatures = [sigma * energies[n] - energies[n + 1] for n in range(5)]

    def product(p, q, table):
        return sum(p[i] * q[j] * table[i + j] for i in range(len(p)) for j in range(len(q)))

    one = jnp.ones((8, LANES), F32)
    none = jnp.zeros((8, LANES), F32)
    smoothed = [one]
    direction = [one]
    result = []
    energy = energies[0]
    for iteration in range(3):
        length = energy / product(direction, direction, curvatures)
        result = [
            (result[i] if i < len(result) else none) + length * direction[i]
            for i in range(len(direction))
        ]
        if iteration < 2:
            image = [sigma * d for d in direction] + [none]
            image = [image[i] - (direction[i - 1] if i else none) for i in range(len(image))]
            smoothed = [
                (smoothed[i] if i < len(smoothed) else none) - length * image[i]
                for i in range(len(image))
            ]
            following = product(smoothed, smoothed, energies)
            ratio = following / energy
            direction = [
                smoothed[i] + (ratio * direction[i] if i < len(direction) else none)
                for i in range(len(smoothed))
            ]
            energy = following
    k0, k1, k2 = result
    return k0 - shift * k1 + shift * shift * k2, k1 - 2.0 * shift * k2, k2


def last_kernel(
    sums_ref, b_ref, x0_ref, x1_ref, x2_ref, y1_ref, y2_ref, y3_ref, solution_hbm, residual_hbm,
    solution_ref, residual_ref, sems
):
    step = ROWS // CHUNKS
    k0, k1, k2 = coefficients([sums_ref[8 * n : 8 * n + 8] for n in range(16)])
    r0, r1, r2 = 1.0 - k0, k0 - k1, k1 - k2

    def copy(i, n):
        src = (solution_ref, residual_ref)[i]
        dst = (solution_hbm, residual_hbm)[i]
        rows = pl.ds(n * step, step)
        return pltpu.make_async_copy(src.at[:, rows, :], dst.at[:, rows, :], sems.at[i, n])

    for n in range(CHUNKS):

        def tile(t, carry):
            at = pl.ds(pl.multiple_of(8 * t - 8, 8), 8)
            wide = pl.ds(pl.multiple_of(8 * t + 8, 8), 8)
            for k in range(LEVELS):
                solution_ref[k, at, :] = (
                    k0 * x0_ref[k, wide, :] + k1 * x1_ref[k, wide, :] + k2 * x2_ref[k, wide, :]
                )
                residual_ref[k, at, :] = (
                    r0 * b_ref[k, at, :] + r1 * y1_ref[k, wide, :]
                    + r2 * y2_ref[k, at, :] + k2 * y3_ref[k, at, :]
                )
            return carry

        lax.fori_loop(1 + n * step // 8, 1 + (n + 1) * step // 8, tile, 0)
        for i in range(2):
            copy(i, n).start()
    for n in range(CHUNKS):
        for i in range(2):
            copy(i, n).wait()


VMEM = pl.BlockSpec(memory_space=pltpu.VMEM)
ANY = pl.BlockSpec(memory_space=pl.ANY)
HBM = pl.BlockSpec(memory_space=pltpu.HBM)


def kept(*shape):
    return pltpu.VMEM(shape, F32)


def call(kernel, outs, ins, in_specs, out_specs=None, scratch=(), limit=8, flops=0, aliases=None):
    return pl.pallas_call(
        kernel,
        out_shape=outs,
        in_specs=in_specs,
        out_specs=[VMEM] * len(outs) if out_specs is None else out_specs,
        scratch_shapes=list(scratch),
        input_output_aliases=aliases or {},
        compiler_params=pltpu.CompilerParams(vmem_limit_bytes=limit * MIB),
        cost_estimate=pl.CostEstimate(flops=flops, bytes_accessed=1000000, transcendentals=0),
        name=kernel.__name__,
    )(*ins)


def on_device(right_side, helmholtz, coupling):
    right_side, helmholtz, coupling = [
        pltpu.with_memory_space_constraint(x, pltpu.HBM) for x in (right_side, helmholtz, coupling)
    ]
    low = pl.BlockSpec((LEVELS, 8, LANES), lambda i: (0, 0, 0))
    high = pl.BlockSpec((LEVELS, 8, LANES), lambda i: (0, ROWS // 8 - 1, 0))
    low_c = pl.BlockSpec((LEVELS - 1, 8, LANES), lambda i: (0, 0, 0))
    high_c = pl.BlockSpec((LEVELS - 1, 8, LANES), lambda i: (0, ROWS // 8 - 1, 0))
    message_rows = -(-(PAD + 3 * STACKED + 5) // 8) * 8
    rows_b, rows_a = pl.pallas_call(
        edge_rows_kernel,
        grid=(1,),
        out_shape=[kept(message_rows, LANES)] * 2,
        in_specs=[low, high, low, high, low_c, high_c],
        out_specs=[pl.BlockSpec((message_rows, LANES), lambda i: (0, 0))] * 2,
        name="edge_rows",
    )(right_side, right_side, helmholtz, helmholtz, coupling, coupling)
    rows_b = swap(rows_b, lat_odd)
    rows_a = swap(rows_a, lat_even)
    field = kept(LEVELS, EXTENDED, LANES)
    block = kept(LEVELS, ROWS, LANES)
    stack = kept(STACKED, 8, LANES)
    edges = kept(LEVELS, 8, LANES)
    message = kept(LANE_MESSAGE, 8, LANES)
    tile_scratch = lambda *n: pltpu.VMEM((*n, 8, LANES), F32)
    b, h, c, last, first, terms = call(
        pack_kernel,
        [block, block, kept(LEVELS - 1, ROWS, LANES), stack, stack, kept(4, 8 * TILES, LANES)],
        [right_side, helmholtz, coupling],
        [HBM] * 3,
        scratch=[pltpu.SemaphoreType.DMA((3, PACKS))],
        flops=10000000,
    )
    halo, lanes_d, lanes_e = call(
        edge_lanes_kernel,
        [kept(2, 4, LEVELS, 8, LANES), message, message],
        [rows_b, rows_a, last, first],
        [VMEM] * 4,
        scratch=[tile_scratch(4, STACKED), tile_scratch(2, 4, LEVELS), tile_scratch(2, 2, LEVELS)],
    )
    scaled, inverse, ratio, x0, edge0, sum0, y1 = call(
        first_kernel,
        [field] * 4 + [edges, kept(8, LANES), field],
        [b, h, c, halo, terms],
        [VMEM] * 5,
        flops=10000000,
    )
    lanes_d = swap(lanes_d, lon_odd)
    lanes_e = swap(lanes_e, lon_even)
    y1, x1, x2, y2, y3, sums = call(
        middle_kernel,
        [field, field, field, block, block, kept(128, LANES)],
        [scaled, inverse, ratio, x0, y1, terms, lanes_d, lanes_e, edge0, sum0],
        [VMEM] * 10,
        scratch=[tile_scratch(LEVELS)] * 5 + [tile_scratch(3, LEVELS)],
        flops=100000000,
        aliases={4: 0},
    )
    sums = lax.all_to_all(sums, AXES, 0, 0, tiled=True)
    result = jax.ShapeDtypeStruct((LEVELS, ROWS, LANES), F32)
    return call(
        last_kernel,
        [result, result],
        [sums, b, x0, x1, x2, y1, y2, y3],
        [VMEM] * 8,
        out_specs=[ANY, ANY],
        scratch=[
            pltpu.VMEM((LEVELS, ROWS, LANES), F32),
            pltpu.VMEM((LEVELS, ROWS, LANES), F32),
            pltpu.SemaphoreType.DMA((2, CHUNKS)),
        ],
        flops=10000000,
    )


def solution(mesh):
    spec = P(None, "lat", "lon")
    return jax.shard_map(
        lambda *args: tuple(on_device(*args)),
        mesh=mesh,
        in_specs=(spec,) * 3,
        out_specs=(spec,) * 2,
        check_vma=False,
    )
```

```python
import functools
import math

import jax
import jax.numpy as jnp
from jax import lax
from jax.experimental import pallas as pl
from jax.experimental.pallas import tpu as pltpu
from jax.sharding import PartitionSpec as P

LEVELS = 20
ROWS = 256
LANES = 128
TOTAL_ROWS = 1024
LON_COEFF = 4.0
TILES = ROWS // 8 + 2
EXTENDED = 8 * TILES + 16
STACKED = 3 * LEVELS - 1
AT_H = LEVELS
AT_C = 2 * LEVELS
CHUNKS = 8
PACKS = 3
GROUP = 16
PARTIALS = 16
PAD = 8
LANE_MESSAGE = LEVELS + (2 * LEVELS + 1) // 3
AXES = ("lon", "lat")
F32 = jnp.float32
MIB = 1 << 20


def swap(x, partner):
    return lax.ppermute(x, AXES, [(i, partner(i)) for i in range(128)])


def lat_even(i):
    return i ^ 1


def lat_odd(i):
    lon, lat = i >> 2, i & 3
    if lat in (1, 2):
        return (lon << 2) | (3 - lat)
    return ((lon ^ 16) << 2) | lat


def lon_even(i):
    return i ^ 4


def lon_odd(i):
    lon, lat = i >> 2, i & 3
    other = (lon + 1) % 32 if lon % 2 else (lon - 1) % 32
    return (other << 2) | lat


def lane_index():
    return lax.broadcasted_iota(jnp.int32, (8, LANES), 1)


def sub_index():
    return lax.broadcasted_iota(jnp.int32, (8, LANES), 0)


def capped_cosine(row):
    angle = (row + 0.5) * (math.pi / TOTAL_ROWS) - 0.5 * math.pi
    square = angle * angle
    value = jnp.full_like(row, 0.0)
    for n in range(8, -1, -1):
        value = value * square + (-1.0) ** n / math.factorial(2 * n)
    return jnp.maximum(value, 0.5)


def row_terms(row):
    here = capped_cosine(row)
    return (
        here,
        LON_COEFF / here,
        (here + capped_cosine(row + 1.0)) * 0.5,
        (here + capped_cosine(row - 1.0)) * 0.5,
    )


def eliminate(tiles):
    count = len(tiles)
    below = [None] * count
    ratio = [None] * count
    value = [None] * count
    total = [None] * count
    for k in range(LEVELS):
        for n, (terms, right, helm, coup, store, put, get) in enumerate(tiles):
            cosine, over, north, south = terms
            pivot = cosine * helm(k) + (2.0 * over + north + south)
            scaled = cosine * coup(k) if k < LEVELS - 1 else None
            if scaled is not None:
                pivot = pivot + scaled
            if k > 0:
                pivot = (pivot + below[n]) - below[n] * ratio[n]
            inverse = 1.0 / pivot
            summed = right(k)
            if k > 0:
                summed = summed + below[n] * value[n]
            value[n] = summed * inverse
            total[n] = summed * value[n] if k == 0 else total[n] + summed * value[n]
            put(k, value[n])
            ratio[n] = scaled * inverse if scaled is not None else None
            below[n] = scaled
            store(k, scaled, inverse, ratio[n])
    for k in range(LEVELS - 2, -1, -1):
        for n, (terms, right, helm, coup, store, put, get) in enumerate(tiles):
            value[n] = get(0, k) + get(1, k) * value[n]
            put(k, value[n])
    return total


def rows_beside(x):
    above = jnp.concatenate([x[1:], pltpu.roll(x, LANES - 3, axis=1)[:1]], 0)
    below = jnp.concatenate([pltpu.roll(x, 3, axis=1)[7:], x[:7]], 0)
    return above, below


def packed_edges(read, lane):
    last = jnp.zeros((8, LANES), F32)
    first = jnp.zeros((8, LANES), F32)
    group = lane // 3
    for t in range(1, TILES - 1):
        turned = pltpu.roll(read(t), 3 * t + 3, axis=1)
        last = jnp.where(group == t, turned, last)
        first = jnp.where(group == t + 1, turned, first)
    return last, first


def edge_rows_kernel(
    b_hbm, h_hbm, c_hbm, o_ref, a_ref, b_lo, b_hi, h_lo, h_hi, c_lo, c_hi, sems
):
    copies = []
    for i, (src, low, high) in enumerate(((b_hbm, b_lo, b_hi), (h_hbm, h_lo, h_hi), (c_hbm, c_lo, c_hi))):
        for n, (dst, at) in enumerate(((low, 0), (high, ROWS - 8))):
            copies.append(pltpu.make_async_copy(src.at[:, pl.ds(at, 8), :], dst, sems.at[i, n]))
            copies[-1].start()
    lat = lax.axis_index("lat")
    even = lat % 2 == 0
    for copy in copies:
        copy.wait()
    levels = [
        (at + k, lo, hi, k)
        for at, count, lo, hi in (
            (0, LEVELS, b_lo, b_hi),
            (AT_H, LEVELS, h_lo, h_hi),
            (AT_C, LEVELS - 1, c_lo, c_hi),
        )
        for k in range(count)
    ]

    def put_high(ref):
        for j, lo, hi, k in reversed(levels):
            ref[pl.ds(PAD + 3 * j - 5, 8), :] = hi[k]

    def put_low(ref):
        for j, lo, hi, k in levels:
            ref[pl.ds(PAD + 3 * j, 8), :] = lo[k]

    @pl.when(even)
    def _():
        put_high(a_ref)

    @pl.when(jnp.logical_not(even))
    def _():
        put_low(a_ref)

    @pl.when(lat == 0)
    def _():
        for j, lo, hi, k in levels:
            for i in range(3):
                o_ref[pl.ds(PAD + 3 * j + i, 1), :] = lo[k, pl.ds(2 - i, 1), :]

    @pl.when(lat == 1)
    def _():
        put_high(o_ref)

    @pl.when(lat == 2)
    def _():
        put_low(o_ref)

    @pl.when(lat == 3)
    def _():
        for j, lo, hi, k in levels:
            for i in range(3):
                o_ref[pl.ds(PAD + 3 * j + i, 1), :] = hi[k, pl.ds(7 - i, 1), :]


def pack_kernel(b_hbm, h_hbm, c_hbm, b_ref, h_ref, c_ref, last_ref, first_ref, terms_ref, sems):
    arrays = (
        (b_hbm, b_ref, 0, LEVELS),
        (h_hbm, h_ref, AT_H, LEVELS),
        (c_hbm, c_ref, AT_C, LEVELS - 1),
    )
    parts = []
    for i, (src, dst, at, count) in enumerate(arrays):
        cuts = (0, 3, count // 2, count) if i == 0 else (0, count // 2, count)
        for n, (lo, hi) in enumerate(zip(cuts, cuts[1:])):
            levels = pl.ds(lo, hi - lo)
            copy = pltpu.make_async_copy(src.at[levels], dst.at[levels], sems.at[i, n])
            copy.start()
            parts.append((copy, dst, at, lo, hi))
    lane = lane_index()
    sub = sub_index()
    base = lax.axis_index("lat") * ROWS
    for n, (copy, source, at, lo, hi) in enumerate(parts):
        copy.wait()
        for t in range(n, TILES, len(parts)):
            for i, term in enumerate(row_terms((base + 8 * t - 8 + sub).astype(F32))):
                terms_ref[i, pl.ds(8 * t, 8), :] = term
        for k in range(lo, hi):
            last, first = packed_edges(lambda t: source[k, pl.ds(8 * t - 8, 8), :], lane)
            last_ref[at + k] = last
            first_ref[at + k] = first


def first_kernel(
    b_ref, h_ref, c_ref, halo_ref, terms_ref, scaled_ref, inverse_ref, ratio_ref, x_ref, edge_ref,
    sum_ref, y_ref
):
    lane = lane_index()
    for n, t in ((0, 0), (1, TILES - 1)):
        for k in range(LEVELS):
            wide = pl.ds(8 * t + 8, 8)
            x_ref[k, wide, :] = halo_ref[n, 0, k]
            inverse_ref[k, wide, :] = halo_ref[n, 2, k]
            if k < LEVELS - 1:
                scaled_ref[k, wide, :] = halo_ref[n, 1, k]
                ratio_ref[k, wide, :] = halo_ref[n, 3, k]

    group = lane // 3
    for k in range(LEVELS):
        edge_ref[k] = jnp.zeros((8, LANES), F32)

    def eliminated(g):
        work = []
        for n in range(4):
            at = pl.ds(pl.multiple_of(32 * g + 8 * n, 8), 8)
            wide = pl.ds(pl.multiple_of(32 * g + 8 * n + 16, 8), 8)
            terms = [
                terms_ref[i, pl.ds(pl.multiple_of(32 * g + 8 * n + 8, 8), 8), :] for i in range(4)
            ]

            def store(k, scaled, inverse, ratio, wide=wide):
                inverse_ref[k, wide, :] = inverse
                if scaled is not None:
                    scaled_ref[k, wide, :] = scaled
                    ratio_ref[k, wide, :] = ratio

            def put(k, value, wide=wide):
                x_ref[k, wide, :] = value

            def get(which, k, wide=wide):
                return (x_ref, ratio_ref)[which][k, wide, :]

            work.append((
                terms,
                lambda k, at=at: b_ref[k, at, :],
                lambda k, at=at: h_ref[k, at, :],
                lambda k, at=at: c_ref[k, at, :],
                store,
                put,
                get,
            ))
        return sum(eliminate(work))

    def neighbours(tiles):
        terms = [
            [terms_ref[i, pl.ds(pl.multiple_of(8 * t, 8), 8), :] for i in range(1, 4)] for t in tiles
        ]
        for k in range(LEVELS):
            edge = edge_ref[k]
            for t, (over, north, south) in zip(tiles, terms):
                start = pl.multiple_of(8 * t + 8, 8)
                wide = pl.ds(start, 8)
                x = x_ref[k, wide, :]
                west = jnp.where(lane == 0, 0.0, pltpu.roll(x, 1, axis=1))
                east = jnp.where(lane == LANES - 1, 0.0, pltpu.roll(x, LANES - 1, axis=1))
                above = x_ref[k, pl.ds(start + 1, 8), :]
                below = x_ref[k, pl.ds(start - 1, 8), :]
                y_ref[k, wide, :] = over * (west + east) + north * above + south * below
                edge = jnp.where(group == t, pltpu.roll(x, 3 * t + 2, axis=1), edge)
            edge_ref[k] = edge

    def both(g, total):
        total = total + eliminated(g)
        neighbours([4 * g - 4 + n for n in range(4)])
        return total

    sum_ref[...] = lax.fori_loop(1, ROWS // 32, both, eliminated(0))
    neighbours(range(TILES - 6, TILES))


def edge_lanes_kernel(
    o_ref, a_ref, last_ref, first_ref, halo_ref, d_ref, e_ref, raw_ref, strip_ref, part_ref
):
    even = lax.axis_index("lat") % 2 == 0
    lon_is_even = lax.axis_index("lon") % 2 == 0
    base = lax.axis_index("lat") * ROWS
    lane = lane_index()
    sub = sub_index()
    group = lane // 3
    slot = lane % 3
    for j in range(STACKED):
        low, high = pl.ds(PAD + 3 * j - 5, 8), pl.ds(PAD + 3 * j, 8)
        south = jnp.where(even, o_ref[low, :], a_ref[low, :])
        north = jnp.where(even, a_ref[high, :], o_ref[high, :])
        raw_ref[0, j] = south
        raw_ref[1, j] = north
        last, first = last_ref[j], first_ref[j]
        for t, value in ((0, south), (TILES - 1, north)):
            turned = pltpu.roll(value, 3 * t + 3, axis=1)
            last = jnp.where(group == t, turned, last)
            first = jnp.where(group == t + 1, turned, first)
        raw_ref[2, j] = last
        raw_ref[3, j] = pltpu.roll(first, LANES - 3, axis=1)
    strip_terms = row_terms((base + 8 * group - 8 + sub).astype(F32))
    work = []
    for n in range(4):
        if n < 2:
            terms = row_terms((base + (TILES - 1) * 8 * n - 8 + sub).astype(F32))
            keep = halo_ref.at[n]
        else:
            terms = strip_terms
            keep = strip_ref.at[n - 2]

        def store(k, scaled, inverse, ratio, keep=keep):
            keep[2, k] = inverse
            if scaled is not None:
                keep[1, k] = scaled
                keep[3, k] = ratio

        def put(k, value, keep=keep):
            keep[0, k] = value

        def get(which, k, keep=keep):
            return keep[3 * which, k]

        work.append((
            terms,
            lambda k, n=n: raw_ref[n, k],
            lambda k, n=n: raw_ref[n, AT_H + k],
            lambda k, n=n: raw_ref[n, AT_C + k],
            store,
            put,
            get,
        ))
    eliminate(work)
    _, over, north, south = strip_terms
    value = [None, None]
    for k in range(LEVELS):
        for side in (0, 1):
            x = strip_ref[side, 0, k]
            up = pltpu.roll(x, 1, axis=1)
            down = pltpu.roll(x, LANES - 1, axis=1)
            if side == 0:
                down = jnp.where(slot == 2, 0.0, down)
            else:
                up = jnp.where(slot == 0, 0.0, up)
            above, below = rows_beside(x)
            y = over * (up + down) + north * above + south * below
            part_ref[side, 0, k] = y
            if k > 0:
                y = y + strip_ref[side, 1, k - 1] * value[side]
            value[side] = y * strip_ref[side, 2, k]
            part_ref[side, 1, k] = value[side]
    for k in range(LEVELS - 1, -1, -1):
        messages = []
        for side in (0, 1):
            if k < LEVELS - 1:
                value[side] = part_ref[side, 1, k] + strip_ref[side, 3, k] * value[side]
            outer = 2 - 2 * side
            known = pltpu.roll(part_ref[side, 0, k], (2 - 2 * outer) % LANES, axis=1)
            message = jnp.where(slot == outer, strip_ref[side, 0, k], known)
            messages.append(jnp.where(slot == 1, value[side], message))
        last, first = messages
        e_ref[k] = jnp.where(lon_is_even, last, first)
        d_ref[k] = jnp.where(lon_is_even, first, last)
    for m in range(LEVELS, LANE_MESSAGE):
        messages = []
        for side in (0, 1):
            outer = 2 - 2 * side
            message = jnp.zeros((8, LANES), F32)
            for q in range(3):
                at = 3 * (m - LEVELS) + q
                source = strip_ref[side, 2, at] if at < LEVELS else strip_ref[side, 1, at - LEVELS]
                message = jnp.where(slot == q, pltpu.roll(source, (q - outer) % LANES, axis=1), message)
            messages.append(message)
        last, first = messages
        e_ref[m] = jnp.where(lon_is_even, last, first)
        d_ref[m] = jnp.where(lon_is_even, first, last)


def middle_kernel(
    scaled_ref, inverse_ref, ratio_ref, x0_ref, y1_in, terms_ref, d_ref, e_ref, edge0_ref, sum_ref,
    y1_ref, x1_ref, x2_ref, y2_ref, y3_ref, sums_ref, strip0_ref, strip_ref, strip2_ref, further_ref,
    edge_ref, factor_ref
):
    del y1_in
    base = lax.axis_index("lat") * ROWS
    lon_is_even = lax.axis_index("lon") % 2 == 0
    lane = lane_index()
    sub = sub_index()
    slot = lane % 3
    group = lane // 3
    _, strip_over, strip_north, strip_south = row_terms((base + 8 * group - 8 + sub).astype(F32))

    def turned(x, by):
        return pltpu.roll(x, by % LANES, axis=1) if by % LANES else x

    def arrived(m):
        e, d = e_ref[m], d_ref[m]
        return jnp.where(lon_is_even, d, e), jnp.where(lon_is_even, e, d)

    for m in range(LEVELS, LANE_MESSAGE):
        left, right = arrived(m)
        for q in range(3):
            at = 3 * (m - LEVELS) + q
            value = jnp.where(slot == 2, turned(left, 2 - q), turned(right, 1 - q))
            if at < LEVELS:
                factor_ref[1, at] = value
            else:
                factor_ref[0, at - LEVELS] = value
    for k in range(LEVELS - 1):
        factor_ref[2, k] = factor_ref[0, k] * factor_ref[1, k]

    def solve_strip(right, out_ref):
        value = None
        for k in range(LEVELS):
            y = right(k)
            if k > 0:
                y = y + factor_ref[0, k - 1] * value
            value = y * factor_ref[1, k]
            out_ref[k] = value
        for k in range(LEVELS - 2, -1, -1):
            value = out_ref[k] + factor_ref[2, k] * value
            out_ref[k] = value

    def first_right(k):
        left, right = arrived(k)
        strip0_ref[k] = jnp.where(slot == 2, left, turned(right, 1))
        further_ref[k] = jnp.where(slot == 2, turned(left, 1), right)
        known = jnp.where(slot == 2, turned(left, 2), turned(right, -1))
        return known + strip_over * edge0_ref[k]

    def second_right(k):
        above, below = rows_beside(strip_ref[k])
        beside = further_ref[k] + edge_ref[k]
        return strip_over * beside + strip_north * above + strip_south * below

    def step(tiles, x_ref, y_ref, out_ref, halo_ref, sums, begun=False):
        starts = [pl.multiple_of(8 * t + 8, 8) for t in tiles]
        wides = [pl.ds(start, 8) for start in starts]
        ats = wides if begun else [pl.ds(pl.multiple_of(8 * t - 8, 8), 8) for t in tiles]
        terms = [
            [terms_ref[i, pl.ds(pl.multiple_of(8 * t, 8), 8), :] for i in range(1, 4)] for t in tiles
        ]
        zero = jnp.zeros((8, LANES), F32)
        cross = [zero] * len(tiles)
        own = [zero] * len(tiles)
        forward = [[] for _ in tiles]
        for k in range(LEVELS):
            for n, t in enumerate(tiles):
                over, north, south = terms[n]
                x = x_ref[k, wides[n], :]
                inject = pltpu.roll(halo_ref[k], 126 - 3 * t, axis=1)
                if begun:
                    inject = jnp.where((lane == 0) | (lane == LANES - 1), inject, 0.0)
                    y = y_ref[k, ats[n], :] + over * inject
                else:
                    west = jnp.where(lane == 0, inject, pltpu.roll(x, 1, axis=1))
                    east = jnp.where(lane == LANES - 1, inject, pltpu.roll(x, LANES - 1, axis=1))
                    above = x_ref[k, pl.ds(starts[n] + 1, 8), :]
                    below = x_ref[k, pl.ds(starts[n] - 1, 8), :]
                    y = over * (west + east) + north * above + south * below
                if sums is not None:
                    y_ref[k, ats[n], :] = y
                    cross[n] = cross[n] + x * y
                if k > 0:
                    y = y + scaled_ref[k - 1, wides[n], :] * forward[n][-1]
                value = y * inverse_ref[k, wides[n], :]
                if sums is not None:
                    own[n] = own[n] + y * value
                forward[n].append(value)
        if out_ref is not None:
            value = [f[-1] for f in forward]
            for k in range(LEVELS - 1, -1, -1):
                edge = edge_ref[k] if begun else None
                for n, t in enumerate(tiles):
                    if k < LEVELS - 1:
                        value[n] = forward[n][k] + ratio_ref[k, wides[n], :] * value[n]
                    out_ref[k, wides[n], :] = value[n]
                    if begun:
                        edge = jnp.where(group == t, pltpu.roll(value[n], 3 * t + 2, axis=1), edge)
                if begun:
                    edge_ref[k] = edge
        if sums is not None:
            return sums[0] + sum(cross), sums[1] + sum(own)

    zero = jnp.zeros((8, LANES), F32)
    totals = [sum_ref[...]]
    for k in range(LEVELS):
        edge_ref[k] = zero
    solve_strip(first_right, strip_ref)
    for x_ref, y_ref, out_ref, halo_ref in (
        (x0_ref, y1_ref, x1_ref, strip0_ref),
        (x1_ref, y2_ref, x2_ref, strip_ref),
        (x2_ref, y3_ref, None, strip2_ref),
    ):
        begun = x_ref is x0_ref
        if out_ref is not None:
            step([0, TILES - 1], x_ref, y_ref, out_ref, halo_ref, None, begun)
        if x_ref is x1_ref:
            solve_strip(second_right, strip2_ref)
        totals += lax.fori_loop(
            0,
            ROWS // 8 // GROUP,
            lambda g, sums: step(
                [GROUP * g + n + 1 for n in range(GROUP)], x_ref, y_ref, out_ref, halo_ref, sums, begun
            ),
            (zero, zero),
        )
    row = zero[:1]
    for n, total in enumerate(totals):
        part = jnp.sum(total, axis=0, keepdims=True)
        for by in (64, 32, 16):
            part = part + pltpu.roll(part, by, axis=1)
        row = jnp.where(lane[:1] // PARTIALS == n, part, row)
    sums_ref[...] = jnp.broadcast_to(row, sums_ref.shape)


def two_sum(a, b):
    total = a + b
    part = total - a
    return total, (a - (total - part)) + (b - part)


def coefficients(parts):
    pairs = [(part, None) for part in parts]
    while len(pairs) > 1:
        joined = []
        for (a, a_low), (b, b_low) in zip(pairs[::2], pairs[1::2]):
            total, error = two_sum(a, b)
            joined.append((total, error if a_low is None else (a_low + b_low) + error))
        pairs = joined
    high, low = pairs[0]
    for axis, by in ((0, 4), (0, 2), (0, 1), (1, 8), (1, 4), (1, 2), (1, 1)):
        by = high.shape[axis] - by
        high, error = two_sum(high, pltpu.roll(high, by, axis=axis))
        low = (low + pltpu.roll(low, by, axis=axis)) + error
    spread = lambda x: jnp.concatenate(
        [jnp.broadcast_to(x[:1, PARTIALS * n : PARTIALS * n + 1], (1, LANES)) for n in range(8)], 0
    )
    high, low = spread(high), spread(low)
    row = lambda x, n: jnp.broadcast_to(x[n : n + 1], (8, LANES))
    shift = jnp.floor(64.0 * (row(high, 1) / row(high, 0)) + 0.5) * (1.0 / 64.0)
    centred = []
    for n in range(7):
        centred.append(row(high, 0) + row(low, 0))
        if n == 6:
            break
        wide = 4097.0 * high
        coarse = wide - (wide - high)
        fine = high - coarse
        following = jnp.concatenate([high[1:], high[:1]], 0)
        rest = jnp.concatenate([low[1:], low[:1]], 0) - shift * low
        total, error = two_sum(following, -shift * coarse)
        rest = rest + error
        total, error = two_sum(total, -shift * fine)
        rest = rest + error
        high = total + rest
        low = rest - (high - total)
    sigma = 1.0 - shift
    energies = [sigma * centred[n] - centred[n + 1] for n in range(6)]
    curvatures = [sigma * energies[n] - energies[n + 1] for n in range(5)]

    def product(p, q, table):
        return sum(p[i] * q[j] * table[i + j] for i in range(len(p)) for j in range(len(q)))

    one = jnp.ones((8, LANES), F32)
    none = jnp.zeros((8, LANES), F32)
    smoothed = [one]
    direction = [one]
    result = []
    energy = energies[0]
    for iteration in range(3):
        length = energy / product(direction, direction, curvatures)
        result = [
            (result[i] if i < len(result) else none) + length * direction[i]
            for i in range(len(direction))
        ]
        if iteration < 2:
            image = [sigma * d for d in direction] + [none]
            image = [image[i] - (direction[i - 1] if i else none) for i in range(len(image))]
            smoothed = [
                (smoothed[i] if i < len(smoothed) else none) - length * image[i]
                for i in range(len(image))
            ]
            following = product(smoothed, smoothed, energies)
            ratio = following / energy
            direction = [
                smoothed[i] + (ratio * direction[i] if i < len(direction) else none)
                for i in range(len(smoothed))
            ]
            energy = following
    k0, k1, k2 = result
    return k0 - shift * k1 + shift * shift * k2, k1 - 2.0 * shift * k2, k2


def last_kernel(
    sums_ref, b_ref, x0_ref, x1_ref, x2_ref, y1_ref, y2_ref, y3_ref, solution_hbm, residual_hbm,
    solution_ref, residual_ref, sems
):
    step = ROWS // CHUNKS
    k0, k1, k2 = coefficients([sums_ref[8 * n : 8 * n + 8] for n in range(16)])
    r0, r1, r2 = 1.0 - k0, k0 - k1, k1 - k2

    def copy(i, n):
        src = (solution_ref, residual_ref)[i]
        dst = (solution_hbm, residual_hbm)[i]
        rows = pl.ds(n * step, step)
        return pltpu.make_async_copy(src.at[:, rows, :], dst.at[:, rows, :], sems.at[i, n])

    for n in range(CHUNKS):

        def tile(t, carry):
            at = pl.ds(pl.multiple_of(8 * t - 8, 8), 8)
            wide = pl.ds(pl.multiple_of(8 * t + 8, 8), 8)
            for k in range(LEVELS):
                solution_ref[k, at, :] = (
                    k0 * x0_ref[k, wide, :] + k1 * x1_ref[k, wide, :] + k2 * x2_ref[k, wide, :]
                )
                residual_ref[k, at, :] = (
                    r0 * b_ref[k, at, :] + r1 * y1_ref[k, wide, :]
                    + r2 * y2_ref[k, at, :] + k2 * y3_ref[k, at, :]
                )
            return carry

        lax.fori_loop(1 + n * step // 8, 1 + (n + 1) * step // 8, tile, 0)
        for i in range(2):
            copy(i, n).start()
    for n in range(CHUNKS):
        for i in range(2):
            copy(i, n).wait()


VMEM = pl.BlockSpec(memory_space=pltpu.VMEM)
ANY = pl.BlockSpec(memory_space=pl.ANY)
HBM = pl.BlockSpec(memory_space=pltpu.HBM)


def kept(*shape):
    return pltpu.VMEM(shape, F32)


def call(kernel, outs, ins, in_specs, out_specs=None, scratch=(), limit=8, flops=0, aliases=None):
    return pl.pallas_call(
        kernel,
        out_shape=outs,
        in_specs=in_specs,
        out_specs=[VMEM] * len(outs) if out_specs is None else out_specs,
        scratch_shapes=list(scratch),
        input_output_aliases=aliases or {},
        compiler_params=pltpu.CompilerParams(vmem_limit_bytes=limit * MIB),
        cost_estimate=pl.CostEstimate(flops=flops, bytes_accessed=1000000, transcendentals=0),
        name=kernel.__name__,
    )(*ins)


def on_device(right_side, helmholtz, coupling):
    right_side, helmholtz, coupling = [
        pltpu.with_memory_space_constraint(x, pltpu.HBM) for x in (right_side, helmholtz, coupling)
    ]
    message_rows = -(-(PAD + 3 * STACKED + 5) // 8) * 8
    tile_scratch = lambda *n: pltpu.VMEM((*n, 8, LANES), F32)
    rows_b, rows_a = call(
        edge_rows_kernel,
        [kept(message_rows, LANES)] * 2,
        [right_side, helmholtz, coupling],
        [HBM] * 3,
        scratch=[tile_scratch(LEVELS)] * 4
        + [tile_scratch(LEVELS - 1)] * 2
        + [pltpu.SemaphoreType.DMA((3, 2))],
    )
    rows_b = swap(rows_b, lat_odd)
    rows_a = swap(rows_a, lat_even)
    field = kept(LEVELS, EXTENDED, LANES)
    block = kept(LEVELS, ROWS, LANES)
    stack = kept(STACKED, 8, LANES)
    edges = kept(LEVELS, 8, LANES)
    message = kept(LANE_MESSAGE, 8, LANES)
    b, h, c, last, first, terms = call(
        pack_kernel,
        [block, block, kept(LEVELS - 1, ROWS, LANES), stack, stack, kept(4, 8 * TILES, LANES)],
        [right_side, helmholtz, coupling],
        [HBM] * 3,
        scratch=[pltpu.SemaphoreType.DMA((3, PACKS))],
        flops=10000000,
    )
    halo, lanes_d, lanes_e = call(
        edge_lanes_kernel,
        [kept(2, 4, LEVELS, 8, LANES), message, message],
        [rows_b, rows_a, last, first],
        [VMEM] * 4,
        scratch=[tile_scratch(4, STACKED), tile_scratch(2, 4, LEVELS), tile_scratch(2, 2, LEVELS)],
    )
    scaled, inverse, ratio, x0, edge0, sum0, y1 = call(
        first_kernel,
        [field] * 4 + [edges, kept(8, LANES), field],
        [b, h, c, halo, terms],
        [VMEM] * 5,
        flops=10000000,
    )
    lanes_d = swap(lanes_d, lon_odd)
    lanes_e = swap(lanes_e, lon_even)
    y1, x1, x2, y2, y3, sums = call(
        middle_kernel,
        [field, field, field, block, block, kept(128, LANES)],
        [scaled, inverse, ratio, x0, y1, terms, lanes_d, lanes_e, edge0, sum0],
        [VMEM] * 10,
        scratch=[tile_scratch(LEVELS)] * 5 + [tile_scratch(3, LEVELS)],
        flops=100000000,
        aliases={4: 0},
    )
    sums = lax.all_to_all(sums, AXES, 0, 0, tiled=True)
    result = jax.ShapeDtypeStruct((LEVELS, ROWS, LANES), F32)
    return call(
        last_kernel,
        [result, result],
        [sums, b, x0, x1, x2, y1, y2, y3],
        [VMEM] * 8,
        out_specs=[ANY, ANY],
        scratch=[
            pltpu.VMEM((LEVELS, ROWS, LANES), F32),
            pltpu.VMEM((LEVELS, ROWS, LANES), F32),
            pltpu.SemaphoreType.DMA((2, CHUNKS)),
        ],
        flops=10000000,
    )


def solution(mesh):
    spec = P(None, "lat", "lon")
    return jax.shard_map(
        lambda *args: tuple(on_device(*args)),
        mesh=mesh,
        in_specs=(spec,) * 3,
        out_specs=(spec,) * 2,
        check_vma=False,
    )
```
